32 devices in a mesh: member: 2 (over x), gx: 16 (over z, y, core).
Axes of the slice: x: 2, y: 2, z: 4, core: 2. Of those that a mesh axis runs over, the one named last changes fastest.
Arguments:
- adj_theta2: float32 [24, 1024, 1024], P('member', 'gx'), parts along dimension 0, may hold values from -6 to 6
- adj_eta: float32 [2048, 1024], P(('member', 'gx')), parts along dimension 0
- diffusivity: bfloat16 [12, 1024, 1024], P(None, 'gx'), may hold values from 0.019897461 to 0.119628906
- land_mask: int32 [12, 1024, 1024], P(None, 'gx'), may hold values 0 or 1
- surface_coef: float32 [1024, 1024], P('gx'), may hold values from 0.02 to 1
- thickness: float32 [12], replicated, may hold values from 0.25 to 1
- seg_perm: int32 [512], replicated, may hold values from 0 to 511, each once
- sponge_width: int32 [4], replicated, may hold values from 2 to 8, as said below
Outputs:
- adj_theta: float32 [24, 1024, 1024], P('member', 'gx'), parts along dimension 0
- adj_free: float32 [2048, 1024], P(('member', 'gx')), parts along dimension 0
- adj_rim: float32 [24, 4096], P('member', 'gx'), parts along dimension 0
The draws below stay inside these ranges and needn't reach their ends.
There are 2 independent parts, one for each index of `member`. The reference program is written for one: setup_inputs(seed, part) draws one part's arguments, and reference() takes and returns one part's arrays. A program takes and returns all parts, laid end to end along the dimension named above; an argument that names none is the same for every part. Nothing has to cross between parts.
Inputs may be any that keep to these rules, and one draw needn't show every extreme that they name: `sponge_width`: each entry is 2 to 8; one side is exactly 8.
All inputs are finite; a program needn't handle non-finite values. No bound on the sum of `land_mask` on one device may be relied on, other than what follows from the above.
Results may differ from the reference program's by a relative error of at most 0.0003.
Values sent between devices are 32-bit elements; how exact they have to be, the bound alone decides.
No kernel may reach another device: no remote copies, remote signals or barrier semaphores. Data moves between devices by JAX's collectives and lax.ppermute only.
A program may use at most 64 MiB of HBM per device.

```python
import math
import jax
import jax.numpy as jnp
from jax import lax

K = 12
NY = 1024
ITERS = 4
WMAX = 8
SEG = 8
NX = 1024
RIM = 4096
NSEG = 512


def draw_adj_eta(key, part):
    key = jax.random.fold_in(key, 11)
    first = jax.random.fold_in(key, 0)
    rows = jnp.arange(NX, dtype=jnp.float32)
    ramp = 1.0 + 2.0 * rows / NX
    values = jax.random.normal(first, (NX, NY), jnp.float32) * ramp[:, None]
    return jnp.clip(values, -12.0, 12.0)


def draw_sponge_width(key, part):
    key = jax.random.fold_in(key, 5)
    first, second = jax.random.split(key)
    widths = jax.random.randint(first, (4,), 2, WMAX + 1)
    side = jax.random.randint(second, (), 0, 4)
    return jnp.where(jnp.arange(4) == side, WMAX, widths).astype(jnp.int32)


def with_ends(array, rng, low, largest):
    shape = array.shape
    spot = [jax.random.randint(jax.random.fold_in(rng, axis), (), 0, shape[axis]) for axis in range(len(shape))]
    array = array.at[tuple(spot)].set(low)
    longest = shape.index(max(shape))
    spot[longest] = (spot[longest] + 1) % shape[longest]
    return array.at[tuple(spot)].set(largest)


def block_levels(own_key, dims, shards, least, high):
    def one(position, parts):
        draws = jax.random.uniform(jax.random.fold_in(jax.random.fold_in(own_key, 6), position), (parts,), jnp.float32, least / len(shards), high / len(shards))
        return jnp.repeat(jnp.exp(draws), dims[position] // parts).reshape((-1,) + (1,) * (len(dims) - position - 1))

    loudness = one(*shards[0])
    for cut in shards[1:]:
        loudness = loudness * one(*cut)
    return loudness


def scatter_about(own_key, dims, spread, reach, cuts=(), kind=jnp.bfloat16):
    drawn = jax.random.normal(own_key, dims, jnp.float32) * spread
    if len(cuts) > 0:
        drawn = block_levels(own_key, dims, cuts, -0.22, 0.18) * drawn
    return jnp.clip(drawn, min=-reach, max=reach).astype(kind)


def setup_inputs(seed: int = 0, part: int = 0) -> dict:
    streams_of = jax.random.split(jax.random.key(seed), 9)
    part_keys = jax.random.split(jax.random.fold_in(streams_of[8], part), 9)
    return {
        "adj_theta2": scatter_about(part_keys[0], (K, NX, NY), 1.0, 6.0, ((1, 16),), jnp.float32),
        "adj_eta": draw_adj_eta(jax.random.fold_in(jax.random.fold_in(streams_of[8], part), 71), part),
        "diffusivity": jnp.clip(jnp.exp(math.log(0.119628906) - 1.7938024 * jax.random.uniform(streams_of[2], (K, NX, NY), jnp.float32) ** block_levels(streams_of[2], (K, NX, NY), ((1, 16),), -0.2, 0.2)), 0.019897461, 0.119628906).astype(jnp.bfloat16),
        "land_mask": with_ends((jax.random.randint(streams_of[3], (K, NX, NY), 0, 8) < 7).astype(jnp.int32), jax.random.fold_in(streams_of[3], 1), 0, 1),
        "surface_coef": jnp.clip(jnp.exp(math.log(1.0) - 3.912023 * jax.random.uniform(streams_of[4], (NX, NY), jnp.float32) ** block_levels(streams_of[4], (NX, NY), ((0, 16),), -0.2, 0.2)), 0.02, 1.0),
        "thickness": jnp.clip(jnp.exp(jax.random.uniform(streams_of[5], (K,), jnp.float32, math.log(0.25), math.log(1.0))), 0.25, 1.0),
        "seg_perm": jax.random.permutation(streams_of[6], NSEG).astype(jnp.int32),
        "sponge_width": draw_sponge_width(jax.random.fold_in(streams_of[8], 71), part),
    }


GMAX = 0.3

def side_rates(sponge_width, first_row, rows, total_rows, total_cols):
    widths = sponge_width.astype(jnp.float32)
    columns = jnp.arange(total_cols, dtype=jnp.int32)
    row_ids = first_row + jnp.arange(rows, dtype=jnp.int32)

    def single(dist, side):
        return jnp.maximum(sponge_width[side] - dist, 0).astype(jnp.float32) * GMAX / widths[side]
    return (single(columns, 0), single(total_cols - 1 - columns, 1), single(row_ids, 2), single(total_rows - 1 - row_ids, 3))

def rim_source(seg_perm, total):
    inverse = jnp.argsort(seg_perm).astype(jnp.int32)
    slots = jnp.arange(total, dtype=jnp.int32)
    return inverse[slots // SEG] * SEG + slots % SEG

def apply_surface(field, surface_coef):
    padded = jnp.pad(field, ((1, 1), (1, 1)))
    beside = padded[2:, 1:-1] + padded[:-2, 1:-1] + padded[1:-1, 2:] + padded[1:-1, :-2]
    return (4.0 + surface_coef) * field - beside

def reference(adj_theta2, adj_eta, diffusivity, land_mask, surface_coef, thickness, seg_perm, sponge_width):
    adj_free = jnp.zeros_like(adj_eta)
    residue = adj_eta
    search = adj_eta
    norm_now = jnp.sum(residue * residue)
    for step in range(ITERS):
        image = apply_surface(search, surface_coef)
        alpha = norm_now / jnp.sum(search * image)
        adj_free = adj_free + alpha * search
        residue = residue - alpha * image
        norm_next = jnp.sum(residue * residue)
        search = residue + norm_next / norm_now * search
        norm_now = norm_next
    wet = land_mask.astype(jnp.float32)
    adj_total = adj_theta2 + thickness[:, None, None] * wet * adj_free[None]
    rate_west, rate_east, rate_south, rate_north = side_rates(sponge_width, 0, NX, NX, NY)
    wet_total = wet * adj_total
    west = lax.optimization_barrier(jnp.sum(wet_total * rate_west[None, None, :], axis=2))
    east = lax.optimization_barrier(jnp.sum(wet_total * rate_east[None, None, :], axis=2))
    south = lax.optimization_barrier(jnp.sum(wet_total * rate_south[None, :, None], axis=1))
    north = lax.optimization_barrier(jnp.sum(wet_total * rate_north[None, :, None], axis=1))
    perim = jnp.concatenate([west, east, south, north], axis=1)
    adj_rim = jnp.take(perim, rim_source(seg_perm, RIM), axis=1)
    gamma = rate_west[None, :] + rate_east[None, :] + rate_south[:, None] + rate_north[:, None]
    adj_one = (1.0 - wet * gamma[None]) * adj_total
    root = wet * jnp.sqrt(diffusivity.astype(jnp.float32))
    scaled = root * adj_one
    padded = jnp.pad(scaled, ((0, 0), (1, 1), (1, 1)))
    beside = padded[:, 2:, 1:-1] + padded[:, :-2, 1:-1] + padded[:, 1:-1, 2:] + padded[:, 1:-1, :-2]
    adj_theta = adj_one + root * (beside - 4.0 * scaled)
    return (adj_theta, adj_free, adj_rim)
```

```python
import functools

import jax
import jax.numpy as jnp
from jax import lax
from jax.experimental import pallas as pl
from jax.experimental.pallas import tpu as pltpu
from jax.sharding import PartitionSpec as P

ITERS = 4
SEG = 8
GMAX = 0.3

CENTER = 4.5
HALF = 4.5
CANCEL = 2000.0

LANES = 128
SUB = 8
PAD = 16
LSLOT = 16

f32 = jnp.float32


def edge_rows(cells, width):
    count = lax.axis_size("gx")
    below = lax.ppermute(cells[-width:], "gx", [(i, i + 1) for i in range(count - 1)])
    above = lax.ppermute(cells[:width], "gx", [(i + 1, i) for i in range(count - 1)])
    return below, above


def apply_surface(field, surface_coef):
    before, after = edge_rows(field, 1)
    padded = jnp.concatenate([before, field, after], axis=0)
    padded = jnp.pad(padded, ((0, 0), (1, 1)))
    beside = padded[2:, 1:-1] + padded[:-2, 1:-1] + padded[1:-1, 2:] + padded[1:-1, :-2]
    return (4.0 + surface_coef) * field - beside


def squares_sum(residue):
    return lax.psum(jnp.sum(residue * residue), "gx")


def plain_solve(adj_eta, surface_coef):
    adj_free = jnp.zeros_like(adj_eta)
    residue = adj_eta
    search = adj_eta
    norm_now = squares_sum(residue)
    for _ in range(ITERS):
        image = apply_surface(search, surface_coef)
        alpha = norm_now / lax.psum(jnp.sum(search * image), "gx")
        adj_free = adj_free + alpha * search
        residue = residue - alpha * image
        norm_next = squares_sum(residue)
        search = residue + norm_next / norm_now * search
        norm_now = norm_next
    before, after = edge_rows(adj_free, 1)
    blank = jnp.zeros((SUB - 1, adj_eta.shape[1]), f32)
    return adj_free, jnp.concatenate([blank, before, after, blank], axis=0)


def beside_tiles(tiles, lane):
    to_east = [pltpu.roll(t, 1, 1) for t in tiles]
    to_west = [pltpu.roll(t, LANES - 1, 1) for t in tiles]
    zero = jnp.zeros_like(tiles[0])
    west = [
        jnp.where(lane == 0, to_east[c - 1] if c else zero, to_east[c]) for c in range(len(tiles))
    ]
    east = [
        jnp.where(lane == LANES - 1, to_west[c + 1] if c + 1 < len(tiles) else zero, to_west[c])
        for c in range(len(tiles))
    ]
    return west, east


def tiles_of(ref, lead, row, count):
    return [ref[(*lead, pl.ds(row, SUB), pl.ds(LANES * c, LANES))] for c in range(count)]


def basis_kernel(eta, coef, first, second, basis, sums, diag):
    me = lax.axis_index("gx")
    count = lax.axis_size("gx")
    rows, cols = eta.shape
    wide = cols // LANES
    even = lax.rem(me, 2) == 0
    reach = ITERS
    basis[0] = jnp.zeros(basis.shape[1:], f32)
    diag[...] = jnp.zeros(diag.shape, f32)
    basis[0, PAD : PAD + rows, :] = eta[...]
    diag[PAD : PAD + rows, :] = (coef[...] - (CENTER - 4.0)) * (1.0 / HALF)
    up = jnp.where(even, second[0 : 2 * reach, :], first[0 : 2 * reach, :])
    down = jnp.where(even, first[0 : 2 * reach, :], second[0 : 2 * reach, :])
    basis[0, PAD - reach : PAD, :] = up[:reach]
    basis[0, PAD + rows : PAD + rows + reach, :] = down[:reach]
    diag[PAD - reach : PAD, :] = (up[reach:] - (CENTER - 4.0)) * (1.0 / HALF)
    diag[PAD + rows : PAD + rows + reach, :] = (down[reach:] - (CENTER - 4.0)) * (1.0 / HALF)
    for k in range(1, ITERS):
        basis[k, 0:SUB, :] = jnp.zeros((SUB, cols), f32)
        basis[k, rows + 2 * PAD - SUB : rows + 2 * PAD, :] = jnp.zeros((SUB, cols), f32)

    keep_up = jnp.where(me > 0, 1.0, 0.0).astype(f32)
    keep_down = jnp.where(me < count - 1, 1.0, 0.0).astype(f32)
    lane = lax.broadcasted_iota(jnp.int32, (SUB, LANES), 1)
    totals = [jnp.zeros((SUB, LANES), f32) for _ in range(2 * ITERS)]
    for k in range(ITERS):
        last = k == ITERS - 1
        own_first, own_last = PAD, PAD + rows - SUB
        starts = range(own_first, own_last + SUB, SUB)
        if not last:
            starts = range(own_first - SUB, own_last + 2 * SUB, SUB)
        for start in starts:
            own = own_first <= start <= own_last
            here = tiles_of(basis, (k,), start, wide)
            north = tiles_of(basis, (k,), start - 1, wide)
            south = tiles_of(basis, (k,), start + 1, wide)
            scale = tiles_of(diag, (), start, wide)
            before = tiles_of(basis, (k - 1,), start, wide) if k else None
            west, east = beside_tiles(here, lane)
            even_sum = jnp.zeros((SUB, LANES), f32)
            odd_sum = jnp.zeros((SUB, LANES), f32)
            for c in range(wide):
                ring = (north[c] + south[c]) + (west[c] + east[c])
                image = scale[c] * here[c] - (1.0 / HALF) * ring
                if k:
                    image = 2.0 * image - before[c]
                if start < own_first:
                    image = image * keep_up
                if start > own_last:
                    image = image * keep_down
                if not last:
                    basis[k + 1, pl.ds(start, SUB), pl.ds(LANES * c, LANES)] = image
                if own:
                    even_sum += here[c] * here[c]
                    odd_sum += here[c] * image
            if own:
                totals[2 * k] += even_sum
                totals[2 * k + 1] += odd_sum
    packed = jnp.concatenate([jnp.sum(t, axis=0, keepdims=True) for t in totals], axis=0)
    for to in range(sums.shape[0]):
        sums[to] = packed


def solve_coefficients(moments):
    scaled = [m / moments[0] for m in moments]
    mu = scaled[:2] + [2.0 * scaled[i] - scaled[i % 2] for i in range(2, 2 * ITERS)]

    def gram(i, j):
        if i == j or abs(i - j) == 1:
            return scaled[i + j]
        return 0.5 * (mu[i + j] + mu[abs(i - j)])

    def image_of(p):
        out = [CENTER * a for a in p] + [None]

        def add(i, v):
            out[i] = v if out[i] is None else out[i] + v

        for i, a in enumerate(p):
            if i == 0:
                add(1, HALF * a)
            else:
                add(i + 1, (0.5 * HALF) * a)
                add(i - 1, (0.5 * HALF) * a)
        return out

    def product(p, q):
        terms = [a * b * gram(i, j) for i, a in enumerate(p) for j, b in enumerate(q)]
        return functools.reduce(jnp.add, terms), functools.reduce(jnp.add, map(jnp.abs, terms))

    def plus(p, scale, q):
        out = []
        for i in range(max(len(p), len(q))):
            if i >= len(q):
                out.append(p[i])
            elif i >= len(p):
                out.append(scale * q[i])
            else:
                out.append(p[i] + scale * q[i])
        return out

    one = jnp.ones_like(moments[0])
    solved, residue, search, norm_now = [], [one], [one], one
    sound = jnp.isfinite(moments[0]) & (moments[0] > 0.0)
    for step in range(ITERS):
        image = image_of(search)
        value, size = product(search, image)
        sound = sound & (size < CANCEL * value)
        alpha = norm_now / value
        solved = plus(solved, alpha, search)
        if step < ITERS - 1:
            residue = plus(residue, -alpha, image)
            norm_next, size = product(residue, residue)
            sound = sound & (size < CANCEL * norm_next)
            search = plus(residue, norm_next / norm_now, search)
            norm_now = norm_next
    return solved, sound


def field_kernel(sums, basis, field, halo, sound_out):
    count = sums.shape[0]
    rows, cols = field.shape
    total = sums[0]
    for source in range(1, count):
        total = total + sums[source]
    across = jnp.sum(total, axis=1, keepdims=True)
    moments = [jnp.broadcast_to(across[m : m + 1, :], (SUB, LANES)) for m in range(2 * ITERS)]
    solved, sound = solve_coefficients(moments)
    sound_out[0] = jnp.min(jnp.where(sound, 1, 0))

    def block(start, c):
        at = (pl.ds(start, SUB), pl.ds(LANES * c, LANES))
        out = solved[0] * basis[(0, *at)]
        for k in range(1, ITERS):
            out = out + solved[k] * basis[(k, *at)]
        return out

    for c in range(cols // LANES):
        cut = pl.ds(LANES * c, LANES)
        halo[0:SUB, cut] = block(PAD - SUB, c)
        halo[SUB : 2 * SUB, cut] = block(PAD + rows, c)
        for start in range(0, rows, SUB):
            field[pl.ds(start, SUB), cut] = block(PAD + start, c)


def tracer_kernel(
    thickness, widths, slot_of, column, field, halo, first, second, theta2, diffusivity, mask,
    out, sent, scaled, roots, edge, sides, ends, lines,
):
    level = pl.program_id(0)
    levels = pl.num_programs(0)
    me = lax.axis_index("gx")
    count = lax.axis_size("gx")
    rows, cols = field.shape
    total_rows = rows * count
    wide = cols // LANES
    even = lax.rem(me, 2) == 0
    lane = lax.broadcasted_iota(jnp.int32, (SUB, LANES), 1)
    sub = lax.broadcasted_iota(jnp.int32, (SUB, LANES), 0)

    def rate(dist, side):
        width = widths[side]
        ramp = jnp.maximum(width - dist, 0).astype(f32)
        return ramp * GMAX / jnp.broadcast_to(width.astype(f32), dist.shape)

    west_rate = rate(lane, 0)
    east_rate = rate(LANES - 1 - lane, 1)
    south_rate = rate(me * rows + sub, 2)
    north_rate = rate((count - 1 - me) * rows + (SUB - 1) - sub, 3)

    @pl.when(level == 0)
    def _():
        depth = column.shape[0]
        at = 2 * ITERS
        for side in range(2):
            mine, other = (second, first) if side == 0 else (first, second)
            theta_row = jnp.where(even, mine[at : at + depth, :], other[at : at + depth, :])
            root_row = jnp.where(
                even, mine[at + depth : at + 2 * depth, :], other[at + depth : at + 2 * depth, :]
            )
            line = SUB - 1 if side == 0 else SUB
            free = halo[line : line + 1, :]
            total = theta_row + jnp.where(root_row > 0.0, column[...] * free, 0.0)
            line_lane = lax.broadcasted_iota(jnp.int32, (depth, cols), 1)
            gamma = rate(line_lane, 0) + rate(cols - 1 - line_lane, 1)
            beyond = root_row * ((1.0 - gamma) * total)
            for l in range(depth):
                edge[side, l] = beyond[l : l + 1, :]

    scaled[SUB - 1 : SUB, :] = edge[0, level]
    scaled[SUB + rows : SUB + rows + 1, :] = edge[1, level]

    def keep_end(which, c, part):
        for low in range(0, LSLOT, SUB):
            at = (which, pl.ds(low, SUB), pl.ds(LANES * c, LANES))
            ends[at] = jnp.where(sub + low == level, part, jnp.where(level == 0, 0.0, ends[at]))

    weight = thickness[level]
    place = lane == sub * LSLOT + level
    for start in range(0, rows, SUB):
        for c in range(wide):
            at = (pl.ds(start, SUB), pl.ds(LANES * c, LANES))
            wet = mask[(0, *at)] != 0
            total = theta2[(0, *at)] + jnp.where(wet, weight * field[at], 0.0)
            gamma = None
            if c == 0:
                gamma = west_rate
                part = jnp.sum(jnp.where(wet, total * west_rate, 0.0), axis=1, keepdims=True)
                kept = jnp.where(level == 0, 0.0, sides[0, pl.ds(start, SUB), :])
                sides[0, pl.ds(start, SUB), :] = jnp.where(place, part, kept)
            if c == wide - 1:
                gamma = east_rate if gamma is None else gamma + east_rate
                part = jnp.sum(jnp.where(wet, total * east_rate, 0.0), axis=1, keepdims=True)
                kept = jnp.where(level == 0, 0.0, sides[1, pl.ds(start, SUB), :])
                sides[1, pl.ds(start, SUB), :] = jnp.where(place, part, kept)
            if start == 0:
                gamma = south_rate if gamma is None else gamma + south_rate
                part = jnp.sum(jnp.where(wet, total * south_rate, 0.0), axis=0, keepdims=True)
                keep_end(0, c, part)
            if start == rows - SUB:
                gamma = north_rate if gamma is None else gamma + north_rate
                part = jnp.sum(jnp.where(wet, total * north_rate, 0.0), axis=0, keepdims=True)
                keep_end(1, c, part)
            one = total if gamma is None else jnp.where(wet, 1.0 - gamma, 1.0) * total
            spread = diffusivity[(0, *at)].astype(f32)
            root = jnp.where(wet, spread * lax.rsqrt(spread), 0.0)
            out[(0, *at)] = one
            roots[at] = root
            scaled[pl.ds(SUB + start, SUB), pl.ds(LANES * c, LANES)] = root * one

    for start in range(0, rows, SUB):
        here = tiles_of(scaled, (), SUB + start, wide)
        north = tiles_of(scaled, (), SUB + start - 1, wide)
        south = tiles_of(scaled, (), SUB + start + 1, wide)
        west, east = beside_tiles(here, lane)
        for c in range(wide):
            at = (pl.ds(start, SUB), pl.ds(LANES * c, LANES))
            ring = (north[c] + south[c]) + (west[c] + east[c])
            out[(0, *at)] += roots[at] * (ring - 4.0 * here[c])

    @pl.when(level == levels - 1)
    def _():
        sent[...] = jnp.zeros(sent.shape, f32)
        own = rows // SEG
        for side in range(2):
            for s in range(own):
                row = jnp.sum(sides[side, pl.ds(SUB * s, SUB), :], axis=0, keepdims=True)
                slot = slot_of[side * (total_rows // SEG) + me * own + s]
                sent[pl.ds(slot, 1), :] = row
        across = cols // SEG
        pick = (
            lax.broadcasted_iota(jnp.int32, (across, cols), 1) // SEG
            == lax.broadcasted_iota(jnp.int32, (across, cols), 0)
        ).astype(f32)

        def end_rows(which):
            values = ends[which]
            phase = lax.rem(lax.broadcasted_iota(jnp.int32, values.shape, 1), SEG)
            stacked = jnp.concatenate(
                [jnp.where(phase == r, values, 0.0) for r in range(SEG)], axis=0
            )
            lines[...] = lax.dot_general(
                pick, stacked, (((1,), (1,)), ((), ())),
                precision=lax.Precision.HIGHEST, preferred_element_type=f32,
            )
            base = 2 * (total_rows // SEG) + which * across

            @pl.loop(0, across)
            def _(s):
                sent[pl.ds(slot_of[base + s], 1), :] = lines[pl.ds(s, 1), :]

        @pl.when(me == 0)
        def _():
            end_rows(0)

        @pl.when(me == count - 1)
        def _():
            end_rows(1)


def rim_kernel(got, rim):
    count, height, _ = got.shape
    levels, width = rim.shape
    total = got[0]
    for source in range(1, count):
        total = total + got[source]
    square = jnp.concatenate([total, jnp.zeros((LANES - height, LANES), f32)], axis=0)
    turned = square.T
    spread = (
        lax.broadcasted_iota(jnp.int32, (LANES, width), 1) // SEG
        == lax.broadcasted_iota(jnp.int32, (LANES, width), 0)
    ).astype(f32)
    wide = jnp.dot(turned, spread, precision=lax.Precision.HIGHEST, preferred_element_type=f32)
    phase = lax.rem(lax.broadcasted_iota(jnp.int32, (LSLOT, width), 1), SEG)
    lines = jnp.zeros((LSLOT, width), f32)
    for r in range(SEG):
        lines = lines + jnp.where(phase == r, wide[LSLOT * r : LSLOT * (r + 1), :], 0.0)
    rim[...] = lines[:levels, :]


def whole(shape):
    return pl.BlockSpec(shape, lambda *_: (0,) * len(shape))


def shards(
    adj_theta2, adj_eta, diffusivity, land_mask, surface_coef, thickness, seg_perm, sponge_width
):
    levels, rows, cols = adj_theta2.shape
    count = lax.axis_size("gx")
    me = lax.axis_index("gx")
    even = lax.rem(me, 2) == 0
    local_segs = (2 * rows * count + 2 * cols) // SEG // count
    slots = -(-local_segs // SUB) * SUB

    def edges(at_end):
        def cut(array, width, dim):
            start = jnp.where(at_end, array.shape[dim] - width, 0)
            return lax.dynamic_slice_in_dim(array, start, width, dim)

        wet = cut(land_mask, 1, 1)[:, 0].astype(f32)
        root = wet * jnp.sqrt(cut(diffusivity, 1, 1)[:, 0].astype(f32))
        return jnp.concatenate(
            [cut(adj_eta, ITERS, 0), cut(surface_coef, ITERS, 0), cut(adj_theta2, 1, 1)[:, 0], root]
        )

    inner = [(i, i ^ 1) for i in range(count)]
    outer = [p for i in range(1, count - 1, 2) for p in ((i, i + 1), (i + 1, i))]
    first = lax.ppermute(edges(even), "gx", inner)
    second = lax.ppermute(edges(jnp.logical_not(even)), "gx", outer)

    vmem = pl.BlockSpec(memory_space=pltpu.VMEM)
    smem = pl.BlockSpec(memory_space=pltpu.SMEM)
    basis, sums = pl.pallas_call(
        basis_kernel,
        out_shape=(
            jax.ShapeDtypeStruct((ITERS, rows + 2 * PAD, cols), f32),
            jax.ShapeDtypeStruct((count, 2 * ITERS, LANES), f32),
        ),
        in_specs=[vmem] * 4,
        out_specs=(vmem, vmem),
        scratch_shapes=[pltpu.VMEM((rows + 2 * PAD, cols), f32)],
        compiler_params=pltpu.CompilerParams(vmem_limit_bytes=32 * 2**20),
        name="basis",
    )(adj_eta, surface_coef, first, second)
    sums = lax.all_to_all(sums, "gx", 0, 0)
    field, halo, sound = pl.pallas_call(
        field_kernel,
        out_shape=(
            jax.ShapeDtypeStruct((rows, cols), f32),
            jax.ShapeDtypeStruct((2 * SUB, cols), f32),
            jax.ShapeDtypeStruct((1,), jnp.int32),
        ),
        in_specs=[vmem] * 2,
        out_specs=(vmem, vmem, smem),
        compiler_params=pltpu.CompilerParams(vmem_limit_bytes=32 * 2**20),
        name="field",
    )(sums, basis)
    field, halo = lax.cond(
        sound[0] > 0,
        lambda *_: (field, halo),
        lambda eta, coef: plain_solve(eta, coef),
        adj_eta,
        surface_coef,
    )
    slot_of = seg_perm // local_segs * slots + seg_perm % local_segs
    level_block = (1, rows, cols)
    edge_shape = first.shape
    adj_theta, sent = pl.pallas_call(
        tracer_kernel,
        grid=(levels,),
        out_shape=(
            jax.ShapeDtypeStruct((levels, rows, cols), f32),
            jax.ShapeDtypeStruct((count * slots, LANES), f32),
        ),
        in_specs=[
            smem,
            smem,
            smem,
            whole((levels, 1)),
            whole((rows, cols)),
            whole((2 * SUB, cols)),
            whole(edge_shape),
            whole(edge_shape),
            pl.BlockSpec(level_block, lambda l: (l, 0, 0)),
            pl.BlockSpec(level_block, lambda l: (l, 0, 0)),
            pl.BlockSpec(level_block, lambda l: (l, 0, 0)),
        ],
        out_specs=(
            pl.BlockSpec(level_block, lambda l: (l, 0, 0)),
            whole((count * slots, LANES)),
        ),
        scratch_shapes=[
            pltpu.VMEM((rows + 2 * SUB, cols), f32),
            pltpu.VMEM((rows, cols), f32),
            pltpu.VMEM((2, levels, 1, cols), f32),
            pltpu.VMEM((2, rows, LANES), f32),
            pltpu.VMEM((2, LSLOT, cols), f32),
            pltpu.VMEM((cols // SEG, LANES), f32),
        ],
        compiler_params=pltpu.CompilerParams(vmem_limit_bytes=32 * 2**20),
        name="tracer",
    )(
        thickness, sponge_width, slot_of, thickness[:, None], field, halo, first, second,
        adj_theta2, diffusivity, land_mask,
    )
    got = lax.all_to_all(sent.reshape(count, slots, LANES), "gx", 0, 0)
    adj_rim = pl.pallas_call(
        rim_kernel,
        out_shape=jax.ShapeDtypeStruct((levels, local_segs * SEG), f32),
        in_specs=[vmem],
        out_specs=vmem,
        compiler_params=pltpu.CompilerParams(vmem_limit_bytes=32 * 2**20),
        name="rim",
    )(got)
    return adj_theta, field, adj_rim


def solution(mesh):
    return jax.shard_map(
        shards,
        mesh=mesh,
        in_specs=(
            P("member", "gx", None),
            P(("member", "gx"), None),
            P(None, "gx", None),
            P(None, "gx", None),
            P("gx", None),
            P(),
            P(),
            P(),
        ),
        out_specs=(P("member", "gx", None), P(("member", "gx"), None), P("member", "gx")),
        check_vma=False,
    )
```

```python
import functools

import jax
import jax.numpy as jnp
from jax import lax
from jax.experimental import pallas as pl
from jax.experimental.pallas import tpu as pltpu
from jax.sharding import PartitionSpec as P

ITERS = 4
SEG = 8
GMAX = 0.3

CENTER = 4.5
HALF = 4.5
CANCEL = 2000.0

LANES = 128
SUB = 8
PAD = 16
LSLOT = 16

f32 = jnp.float32


def edge_rows(cells, width):
    count = lax.axis_size("gx")
    below = lax.ppermute(cells[-width:], "gx", [(i, i + 1) for i in range(count - 1)])
    above = lax.ppermute(cells[:width], "gx", [(i + 1, i) for i in range(count - 1)])
    return below, above


def apply_surface(field, surface_coef):
    before, after = edge_rows(field, 1)
    padded = jnp.concatenate([before, field, after], axis=0)
    padded = jnp.pad(padded, ((0, 0), (1, 1)))
    beside = padded[2:, 1:-1] + padded[:-2, 1:-1] + padded[1:-1, 2:] + padded[1:-1, :-2]
    return (4.0 + surface_coef) * field - beside


def squares_sum(residue):
    return lax.psum(jnp.sum(residue * residue), "gx")


def plain_solve(adj_eta, surface_coef):
    adj_free = jnp.zeros_like(adj_eta)
    residue = adj_eta
    search = adj_eta
    norm_now = squares_sum(residue)
    for _ in range(ITERS):
        image = apply_surface(search, surface_coef)
        alpha = norm_now / lax.psum(jnp.sum(search * image), "gx")
        adj_free = adj_free + alpha * search
        residue = residue - alpha * image
        norm_next = squares_sum(residue)
        search = residue + norm_next / norm_now * search
        norm_now = norm_next
    before, after = edge_rows(adj_free, 1)
    blank = jnp.zeros((SUB - 1, adj_eta.shape[1]), f32)
    return adj_free, jnp.concatenate([blank, before, after, blank], axis=0)


def beside_tiles(tiles, lane):
    to_east = [pltpu.roll(t, 1, 1) for t in tiles]
    to_west = [pltpu.roll(t, LANES - 1, 1) for t in tiles]
    zero = jnp.zeros_like(tiles[0])
    west = [
        jnp.where(lane == 0, to_east[c - 1] if c else zero, to_east[c]) for c in range(len(tiles))
    ]
    east = [
        jnp.where(lane == LANES - 1, to_west[c + 1] if c + 1 < len(tiles) else zero, to_west[c])
        for c in range(len(tiles))
    ]
    return west, east


def tiles_of(ref, lead, row, count):
    return [ref[(*lead, pl.ds(row, SUB), pl.ds(LANES * c, LANES))] for c in range(count)]


def next_tiles(here, north, south, scale, before, lane):
    west, east = beside_tiles(here, lane)
    out = []
    for c in range(len(here)):
        ring = (north[c] + south[c]) + (west[c] + east[c])
        image = scale[c] * here[c] - (1.0 / HALF) * ring
        out.append(image if before is None else 2.0 * image - before[c])
    return out


def products(here, after):
    return (
        functools.reduce(jnp.add, [a * a for a in here]),
        functools.reduce(jnp.add, [a * b for a, b in zip(here, after, strict=True)]),
    )


def centred(coef):
    return (coef - (CENTER - 4.0)) * (1.0 / HALF)


def inner_kernel(eta, coef, inner, partial, diag):
    rows, cols = eta.shape
    wide = cols // LANES
    lane = lax.broadcasted_iota(jnp.int32, (SUB, LANES), 1)
    inner[0, SUB : SUB + rows, :] = eta[...]
    diag[...] = centred(coef[...])
    for k in range(ITERS):
        inner[k, 0:SUB, :] = jnp.zeros((SUB, cols), f32)
        inner[k, SUB + rows : 2 * SUB + rows, :] = jnp.zeros((SUB, cols), f32)
    totals = [jnp.zeros((SUB, LANES), f32) for _ in range(2 * ITERS)]
    for k in range(ITERS):
        last = k == ITERS - 1
        for start in range(SUB, rows, SUB) if last else range(0, rows, SUB):
            counted = SUB <= start < rows - SUB
            if last and not counted:
                continue
            here = tiles_of(inner, (k,), SUB + start, wide)
            north = tiles_of(inner, (k,), SUB + start - 1, wide)
            south = tiles_of(inner, (k,), SUB + start + 1, wide)
            before = tiles_of(inner, (k - 1,), SUB + start, wide) if k else None
            after = next_tiles(here, north, south, tiles_of(diag, (), start, wide), before, lane)
            if not last:
                for c in range(wide):
                    inner[k + 1, pl.ds(SUB + start, SUB), pl.ds(LANES * c, LANES)] = after[c]
            if counted:
                even_sum, odd_sum = products(here, after)
                totals[2 * k] += even_sum
                totals[2 * k + 1] += odd_sum
    for i, total in enumerate(totals):
        partial[i] = total


def outer_kernel(eta, coef, inner, partial, first, second, edge, sums, diag):
    me = lax.axis_index("gx")
    count = lax.axis_size("gx")
    rows, cols = eta.shape
    wide = cols // LANES
    even = lax.rem(me, 2) == 0
    lane = lax.broadcasted_iota(jnp.int32, (SUB, LANES), 1)
    totals = [partial[i] for i in range(2 * ITERS)]
    zeros = jnp.zeros((SUB, cols), f32)
    up = jnp.where(even, second[...], first[...])
    down = jnp.where(even, first[...], second[...])
    for side in range(2):
        own = 2 * SUB if side == 0 else SUB
        beyond = SUB if side == 0 else 2 * SUB
        outside = 0 if side == 0 else 3 * SUB
        beside = 3 * SUB if side == 0 else 0
        line = 0 if side == 0 else rows - SUB
        beside_line = SUB if side == 0 else rows - 2 * SUB
        got = up if side == 0 else down
        exists = jnp.where((me > 0) if side == 0 else (me < count - 1), 1.0, 0.0).astype(f32)
        for k in range(ITERS):
            edge[k, side, pl.ds(outside, SUB), :] = zeros
            edge[k, side, pl.ds(beside, SUB), :] = inner[k, pl.ds(SUB + beside_line, SUB), :]
        blank = jnp.zeros((SUB - ITERS, cols), f32)
        if side == 0:
            eta_got = jnp.concatenate([blank, got[:ITERS]], axis=0)
            coef_got = jnp.concatenate([blank, got[ITERS:]], axis=0)
        else:
            eta_got = jnp.concatenate([got[:ITERS], blank], axis=0)
            coef_got = jnp.concatenate([got[ITERS:], blank], axis=0)
        edge[0, side, pl.ds(beyond, SUB), :] = eta_got
        edge[0, side, pl.ds(own, SUB), :] = eta[pl.ds(line, SUB), :]
        diag[side, pl.ds(beyond, SUB), :] = centred(coef_got)
        diag[side, pl.ds(own, SUB), :] = centred(coef[pl.ds(line, SUB), :])
        for k in range(ITERS):
            last = k == ITERS - 1
            for start in (own,) if last else (own, beyond):
                here = tiles_of(edge, (k, side), start, wide)
                north = tiles_of(edge, (k, side), start - 1, wide)
                south = tiles_of(edge, (k, side), start + 1, wide)
                before = tiles_of(edge, (k - 1, side), start, wide) if k else None
                scale = tiles_of(diag, (side,), start, wide)
                after = next_tiles(here, north, south, scale, before, lane)
                if start == beyond:
                    after = [a * exists for a in after]
                if not last:
                    for c in range(wide):
                        at = (pl.ds(start, SUB), pl.ds(LANES * c, LANES))
                        edge[(k + 1, side, *at)] = after[c]
                if start == own:
                    even_sum, odd_sum = products(here, after)
                    totals[2 * k] += even_sum
                    totals[2 * k + 1] += odd_sum
    packed = jnp.concatenate([jnp.sum(t, axis=0, keepdims=True) for t in totals], axis=0)
    for to in range(sums.shape[0]):
        sums[to] = packed


def solve_coefficients(moments):
    scaled = [m / moments[0] for m in moments]
    mu = scaled[:2] + [2.0 * scaled[i] - scaled[i % 2] for i in range(2, 2 * ITERS)]

    def gram(i, j):
        if i == j or abs(i - j) == 1:
            return scaled[i + j]
        return 0.5 * (mu[i + j] + mu[abs(i - j)])

    def image_of(p):
        out = [CENTER * a for a in p] + [None]

        def add(i, v):
            out[i] = v if out[i] is None else out[i] + v

        for i, a in enumerate(p):
            if i == 0:
                add(1, HALF * a)
            else:
                add(i + 1, (0.5 * HALF) * a)
                add(i - 1, (0.5 * HALF) * a)
        return out

    def product(p, q):
        terms = [a * b * gram(i, j) for i, a in enumerate(p) for j, b in enumerate(q)]
        return functools.reduce(jnp.add, terms), functools.reduce(jnp.add, map(jnp.abs, terms))

    def plus(p, scale, q):
        out = []
        for i in range(max(len(p), len(q))):
            if i >= len(q):
                out.append(p[i])
            elif i >= len(p):
                out.append(scale * q[i])
            else:
                out.append(p[i] + scale * q[i])
        return out

    one = jnp.ones_like(moments[0])
    solved, residue, search, norm_now = [], [one], [one], one
    sound = jnp.isfinite(moments[0]) & (moments[0] > 0.0)
    for step in range(ITERS):
        image = image_of(search)
        value, size = product(search, image)
        sound = sound & (size < CANCEL * value)
        alpha = norm_now / value
        solved = plus(solved, alpha, search)
        if step < ITERS - 1:
            residue = plus(residue, -alpha, image)
            norm_next, size = product(residue, residue)
            sound = sound & (size < CANCEL * norm_next)
            search = plus(residue, norm_next / norm_now, search)
            norm_now = norm_next
    return solved, sound


def rate(dist, widths, side):
    width = widths[side]
    ramp = jnp.maximum(width - dist, 0).astype(f32)
    return ramp * GMAX / jnp.broadcast_to(width.astype(f32), dist.shape)


def tile_iotas():
    lane = lax.broadcasted_iota(jnp.int32, (SUB, LANES), 1)
    sub = lax.broadcasted_iota(jnp.int32, (SUB, LANES), 0)
    return lane, sub


def side_rates(widths, me, count, rows):
    lane, sub = tile_iotas()
    return (
        rate(lane, widths, 0),
        rate(LANES - 1 - lane, widths, 1),
        rate(me * rows + sub, widths, 2),
        rate((count - 1 - me) * rows + (SUB - 1) - sub, widths, 3),
    )


def strip_kernel(
    thickness, widths, _order, theta2, diffusivity, mask,
    near, far, side_part, side_weight, end_part, end_weight,
    theta_ends, mask_ends, spread_ends, theta_sides, mask_sides, sems,
):
    levels, rows, cols = theta2.shape
    me = lax.axis_index("gx")
    count = lax.axis_size("gx")
    even = lax.rem(me, 2) == 0
    wide = cols // LANES
    half = spread_ends.shape[2]
    copies = []
    for e in range(2):
        ends = pl.ds(0 if e == 0 else rows - SUB, SUB)
        thick = pl.ds(0 if e == 0 else rows - half, half)
        lanes = pl.ds(0 if e == 0 else cols - LANES, LANES)
        copies += [
            pltpu.make_async_copy(theta2.at[:, ends, :], theta_ends.at[e], sems.at[5 * e]),
            pltpu.make_async_copy(mask.at[:, ends, :], mask_ends.at[e], sems.at[5 * e + 1]),
            pltpu.make_async_copy(diffusivity.at[:, thick, :], spread_ends.at[e], sems.at[5 * e + 2]),
            pltpu.make_async_copy(theta2.at[:, :, lanes], theta_sides.at[e], sems.at[5 * e + 3]),
            pltpu.make_async_copy(mask.at[:, :, lanes], mask_sides.at[e], sems.at[5 * e + 4]),
        ]
    for copy in copies:
        copy.start()
    for copy in copies:
        copy.wait()

    lane, sub = tile_iotas()
    rates = side_rates(widths, me, count, rows)
    for l in range(levels):
        rows_of = []
        for e in range(2):
            line = 0 if e == 0 else SUB - 1
            deep = 0 if e == 0 else half - 1
            wet = mask_ends[e, l, line : line + 1, :] != 0
            spread = spread_ends[e, l, :, :].astype(f32)[deep : deep + 1, :]
            root = jnp.where(wet, spread * lax.rsqrt(spread), 0.0)
            rows_of.append((theta_ends[e, l, line : line + 1, :], root))
        for i in range(2):
            near[levels * i + l : levels * i + l + 1, :] = jnp.where(even, rows_of[1][i], rows_of[0][i])
            far[levels * i + l : levels * i + l + 1, :] = jnp.where(even, rows_of[0][i], rows_of[1][i])
    for side in range(2):
        for start in range(0, rows, SUB):
            kept = jnp.zeros((SUB, LANES), f32)
            for l in range(levels):
                at = (side, l, pl.ds(start, SUB), slice(None))
                wet_rate = jnp.where(mask_sides[at] != 0, rates[side], 0.0)
                part = jnp.sum(theta_sides[at] * wet_rate, axis=1, keepdims=True)
                kept = jnp.where(lane == sub * LSLOT + l, part, kept)
                side_weight[at] = thickness[l] * wet_rate
            side_part[side, pl.ds(start, SUB), :] = kept

    def end(e):
        for c in range(wide):
            cut = pl.ds(LANES * c, LANES)
            for low in range(0, LSLOT, SUB):
                kept = jnp.zeros((SUB, LANES), f32)
                for l in range(low, min(low + SUB, levels)):
                    wet_rate = jnp.where(mask_ends[e, l, :, cut] != 0, rates[2 + e], 0.0)
                    part = jnp.sum(theta_ends[e, l, :, cut] * wet_rate, axis=0, keepdims=True)
                    kept = jnp.where(sub + low == l, part, kept)
                    end_weight[e, l, :, cut] = thickness[l] * wet_rate
                end_part[e, pl.ds(low, SUB), cut] = kept

    @pl.when(me == 0)
    def _():
        end(0)

    @pl.when(me == count - 1)
    def _():
        end(1)


def fill_sent(slot_of, field, side_part, side_weight, end_part, end_weight, sent, ends, lines):
    rows, cols = field.shape
    levels = side_weight.shape[1]
    me = lax.axis_index("gx")
    count = lax.axis_size("gx")
    total_rows = rows * count
    lane, sub = tile_iotas()
    sent[...] = jnp.zeros(sent.shape, f32)
    own = rows // SEG
    for side in range(2):
        cut = pl.ds(0 if side == 0 else cols - LANES, LANES)
        for s in range(own):
            at = pl.ds(SUB * s, SUB)
            free = field[at, cut]
            kept = jnp.zeros((SUB, LANES), f32)
            for l in range(levels):
                part = jnp.sum(side_weight[side, l, at, :] * free, axis=1, keepdims=True)
                kept = jnp.where(lane == sub * LSLOT + l, part, kept)
            row = jnp.sum(kept + side_part[side, at, :], axis=0, keepdims=True)
            slot = slot_of[side * (total_rows // SEG) + me * own + s]
            sent[pl.ds(slot, 1), :] = row
    across = cols // SEG

    def end_rows(e):
        for c in range(cols // LANES):
            cut = pl.ds(LANES * c, LANES)
            free = field[pl.ds(0 if e == 0 else rows - SUB, SUB), cut]
            for low in range(0, LSLOT, SUB):
                kept = end_part[e, pl.ds(low, SUB), cut]
                for l in range(low, min(low + SUB, levels)):
                    part = jnp.sum(end_weight[e, l, :, cut] * free, axis=0, keepdims=True)
                    kept = jnp.where(sub + low == l, kept + part, kept)
                ends[pl.ds(low, SUB), cut] = kept
        values = ends[...]
        phase = lax.rem(lax.broadcasted_iota(jnp.int32, values.shape, 1), SEG)
        stacked = jnp.concatenate([jnp.where(phase == r, values, 0.0) for r in range(SEG)], axis=0)
        pick = (
            lax.broadcasted_iota(jnp.int32, (across, cols), 1) // SEG
            == lax.broadcasted_iota(jnp.int32, (across, cols), 0)
        ).astype(f32)
        lines[...] = lax.dot_general(
            pick, stacked, (((1,), (1,)), ((), ())),
            precision=lax.Precision.HIGHEST, preferred_element_type=f32,
        )
        base = 2 * (total_rows // SEG) + e * across

        @pl.loop(0, across)
        def _(s):
            sent[pl.ds(slot_of[base + s], 1), :] = lines[pl.ds(s, 1), :]

    @pl.when(me == 0)
    def _():
        end_rows(0)

    @pl.when(me == count - 1)
    def _():
        end_rows(1)


def field_kernel(
    slot_of, sums, inner, edge, side_part, side_weight, end_part, end_weight,
    field, halo, sent, sound_out, ends, lines,
):
    count = sums.shape[0]
    rows, cols = field.shape
    total = sums[0]
    for source in range(1, count):
        total = total + sums[source]
    across = jnp.sum(total, axis=1, keepdims=True)
    moments = [jnp.broadcast_to(across[m : m + 1, :], (SUB, LANES)) for m in range(2 * ITERS)]
    solved, sound = solve_coefficients(moments)
    sound_out[0] = jnp.min(jnp.where(sound, 1, 0))

    def mixed(parts):
        return functools.reduce(jnp.add, [a * p for a, p in zip(solved, parts, strict=True)])

    for c in range(cols // LANES):
        cut = pl.ds(LANES * c, LANES)

        def at_edge(side, row):
            return mixed([edge[k, side, pl.ds(row, SUB), cut] for k in range(ITERS)])

        halo[0:SUB, cut] = at_edge(0, SUB)
        field[0:SUB, cut] = at_edge(0, 2 * SUB)
        field[rows - SUB : rows, cut] = at_edge(1, SUB)
        halo[SUB : 2 * SUB, cut] = at_edge(1, 2 * SUB)
        for start in range(SUB, rows - SUB, SUB):
            at = pl.ds(SUB + start, SUB)
            field[pl.ds(start, SUB), cut] = mixed([inner[k, at, cut] for k in range(ITERS)])
    fill_sent(slot_of, field, side_part, side_weight, end_part, end_weight, sent, ends, lines)


def tracer_kernel(
    thickness, widths, column, field, halo, near, far, theta2, diffusivity, mask,
    out, scaled, roots, beyond,
):
    level = pl.program_id(0)
    me = lax.axis_index("gx")
    count = lax.axis_size("gx")
    rows, cols = field.shape
    wide = cols // LANES
    even = lax.rem(me, 2) == 0
    lane, _ = tile_iotas()
    west_rate, east_rate, south_rate, north_rate = side_rates(widths, me, count, rows)

    @pl.when(level == 0)
    def _():
        depth = column.shape[0]
        for side in range(2):
            mine, other = (far, near) if side == 0 else (near, far)
            theta_row = jnp.where(even, mine[0:depth, :], other[0:depth, :])
            root_row = jnp.where(even, mine[depth : 2 * depth, :], other[depth : 2 * depth, :])
            line = SUB - 1 if side == 0 else SUB
            free = halo[line : line + 1, :]
            total = theta_row + jnp.where(root_row > 0.0, column[...] * free, 0.0)
            line_lane = lax.broadcasted_iota(jnp.int32, (depth, cols), 1)
            gamma = rate(line_lane, widths, 0) + rate(cols - 1 - line_lane, widths, 1)
            lines = root_row * ((1.0 - gamma) * total)
            for l in range(depth):
                beyond[side, l] = lines[l : l + 1, :]

    scaled[SUB - 1 : SUB, :] = beyond[0, level]
    scaled[SUB + rows : SUB + rows + 1, :] = beyond[1, level]

    weight = thickness[level]
    for start in range(0, rows, SUB):
        for c in range(wide):
            at = (pl.ds(start, SUB), pl.ds(LANES * c, LANES))
            wet = mask[(0, *at)] != 0
            total = theta2[(0, *at)] + jnp.where(wet, weight * field[at], 0.0)
            parts = [
                r
                for r, there in (
                    (west_rate, c == 0),
                    (east_rate, c == wide - 1),
                    (south_rate, start == 0),
                    (north_rate, start == rows - SUB),
                )
                if there
            ]
            one = total
            if parts:
                one = jnp.where(wet, 1.0 - functools.reduce(jnp.add, parts), 1.0) * total
            spread = diffusivity[(0, *at)].astype(f32)
            root = jnp.where(wet, spread * lax.rsqrt(spread), 0.0)
            out[(0, *at)] = one
            roots[at] = root
            scaled[pl.ds(SUB + start, SUB), pl.ds(LANES * c, LANES)] = root * one

    for start in range(0, rows, SUB):
        here = tiles_of(scaled, (), SUB + start, wide)
        north = tiles_of(scaled, (), SUB + start - 1, wide)
        south = tiles_of(scaled, (), SUB + start + 1, wide)
        west, east = beside_tiles(here, lane)
        for c in range(wide):
            at = (pl.ds(start, SUB), pl.ds(LANES * c, LANES))
            ring = (north[c] + south[c]) + (west[c] + east[c])
            out[(0, *at)] += roots[at] * (ring - 4.0 * here[c])


def rim_kernel(got, rim):
    count, height, _ = got.shape
    levels, width = rim.shape
    total = got[0]
    for source in range(1, count):
        total = total + got[source]
    square = jnp.concatenate([total, jnp.zeros((LANES - height, LANES), f32)], axis=0)
    turned = square.T
    spread = (
        lax.broadcasted_iota(jnp.int32, (LANES, width), 1) // SEG
        == lax.broadcasted_iota(jnp.int32, (LANES, width), 0)
    ).astype(f32)
    wide = jnp.dot(turned, spread, precision=lax.Precision.HIGHEST, preferred_element_type=f32)
    phase = lax.rem(lax.broadcasted_iota(jnp.int32, (LSLOT, width), 1), SEG)
    lines = jnp.zeros((LSLOT, width), f32)
    for r in range(SEG):
        lines = lines + jnp.where(phase == r, wide[LSLOT * r : LSLOT * (r + 1), :], 0.0)
    rim[...] = lines[:levels, :]


VMEM = pl.BlockSpec(memory_space=pltpu.VMEM)
SMEM = pl.BlockSpec(memory_space=pltpu.SMEM)
ANY = pl.BlockSpec(memory_space=pl.ANY)


def whole(shape):
    return pl.BlockSpec(shape, lambda *_: (0,) * len(shape))


def local_call(kernel, name, outs, ins, out_specs=None, scratch=(), **more):
    return pl.pallas_call(
        kernel,
        out_shape=tuple(jax.ShapeDtypeStruct(*o) if isinstance(o, tuple) else o for o in outs),
        in_specs=ins,
        out_specs=out_specs or tuple(VMEM for _ in outs),
        scratch_shapes=list(scratch),
        compiler_params=pltpu.CompilerParams(vmem_limit_bytes=32 * 2**20),
        name=name,
        **more,
    )


def shards(
    adj_theta2, adj_eta, diffusivity, land_mask, surface_coef, thickness, seg_perm, sponge_width
):
    levels, rows, cols = adj_theta2.shape
    count = lax.axis_size("gx")
    me = lax.axis_index("gx")
    even = lax.rem(me, 2) == 0
    local_segs = (2 * rows * count + 2 * cols) // SEG // count
    slots = -(-local_segs // SUB) * SUB
    slot_of = seg_perm // local_segs * slots + seg_perm % local_segs
    inner_pairs = [(i, i ^ 1) for i in range(count)]
    outer_pairs = [p for i in range(1, count - 1, 2) for p in ((i, i + 1), (i + 1, i))]

    def edges(at_end):
        start = jnp.where(at_end, rows - ITERS, 0)
        return jnp.concatenate(
            [lax.dynamic_slice_in_dim(a, start, ITERS, 0) for a in (adj_eta, surface_coef)]
        )

    first = lax.ppermute(edges(even), "gx", inner_pairs)
    second = lax.ppermute(edges(jnp.logical_not(even)), "gx", outer_pairs)

    inner, partial = local_call(
        inner_kernel,
        "inner",
        [((ITERS, rows + 2 * SUB, cols), f32), ((2 * ITERS, SUB, LANES), f32)],
        [VMEM] * 2,
        scratch=[pltpu.VMEM((rows, cols), f32)],
        cost_estimate=pl.CostEstimate(flops=10**6, bytes_accessed=10**6, transcendentals=0),
    )(adj_eta, surface_coef)
    edge, sums = local_call(
        outer_kernel,
        "outer",
        [((ITERS, 2, 4 * SUB, cols), f32), ((count, 2 * ITERS, LANES), f32)],
        [VMEM] * 6,
        scratch=[pltpu.VMEM((2, 4 * SUB, cols), f32)],
    )(adj_eta, surface_coef, inner, partial, first, second)
    all_sums = lax.all_to_all(sums, "gx", 0, 0)

    near, far, *strips = local_call(
        strip_kernel,
        "strip",
        [
            ((2 * levels, cols), f32),
            ((2 * levels, cols), f32),
            ((2, rows, LANES), f32),
            ((2, levels, rows, LANES), f32),
            ((2, LSLOT, cols), f32),
            ((2, levels, SUB, cols), f32),
        ],
        [SMEM, SMEM, ANY, ANY, ANY, ANY],
        scratch=[
            pltpu.VMEM((2, levels, SUB, cols), f32),
            pltpu.VMEM((2, levels, SUB, cols), jnp.int32),
            pltpu.VMEM((2, levels, 2 * SUB, cols), diffusivity.dtype),
            pltpu.VMEM((2, levels, rows, LANES), f32),
            pltpu.VMEM((2, levels, rows, LANES), jnp.int32),
            pltpu.SemaphoreType.DMA((10,)),
        ],
        cost_estimate=pl.CostEstimate(flops=10**6, bytes_accessed=4 * 10**6, transcendentals=0),
    )(thickness, sponge_width, sums, adj_theta2, diffusivity, land_mask)
    near = lax.ppermute(near, "gx", inner_pairs)
    far = lax.ppermute(far, "gx", outer_pairs)

    sent_shape = ((count * slots, LANES), f32)
    sent_scratch = [pltpu.VMEM((LSLOT, cols), f32), pltpu.VMEM((cols // SEG, LANES), f32)]
    field, halo, sent, sound = local_call(
        field_kernel,
        "field",
        [((rows, cols), f32), ((2 * SUB, cols), f32), sent_shape, ((1,), jnp.int32)],
        [SMEM] + [VMEM] * 7,
        out_specs=(VMEM, VMEM, VMEM, SMEM),
        scratch=sent_scratch,
    )(slot_of, all_sums, inner, edge, *strips)

    def route(rows_out):
        got = lax.all_to_all(rows_out.reshape(count, slots, LANES), "gx", 0, 0)
        (adj_rim,) = local_call(
            rim_kernel, "rim", [((levels, local_segs * SEG), f32)], [VMEM]
        )(got)
        return adj_rim

    level_block = pl.BlockSpec((1, rows, cols), lambda l: (l, 0, 0))

    def tracer(free, beyond):
        (adj_theta,) = local_call(
            tracer_kernel,
            "tracer",
            [((levels, rows, cols), f32)],
            [
                SMEM,
                SMEM,
                whole((levels, 1)),
                whole((rows, cols)),
                whole((2 * SUB, cols)),
                whole(near.shape),
                whole(far.shape),
                level_block,
                level_block,
                level_block,
            ],
            out_specs=(level_block,),
            scratch=[
                pltpu.VMEM((rows + 2 * SUB, cols), f32),
                pltpu.VMEM((rows, cols), f32),
                pltpu.VMEM((2, levels, 1, cols), f32),
            ],
            grid=(levels,),
            cost_estimate=pl.CostEstimate(
                flops=24 * 10**6, bytes_accessed=12 * 10**6, transcendentals=10**6
            ),
        )(
            thickness, sponge_width, thickness[:, None], free, beyond, near, far,
            adj_theta2, diffusivity, land_mask,
        )
        return adj_theta

    adj_rim = route(sent)
    adj_theta = tracer(field, halo)

    def again():
        free, beyond = plain_solve(adj_eta, surface_coef)
        (rows_out,) = local_call(
            fill_sent, "refill", [sent_shape], [SMEM] + [VMEM] * 5, scratch=sent_scratch
        )(slot_of, free, *strips)
        return tracer(free, beyond), free, route(rows_out)

    return lax.cond(sound[0] > 0, lambda: (adj_theta, field, adj_rim), again)


def solution(mesh):
    return jax.shard_map(
        shards,
        mesh=mesh,
        in_specs=(
            P("member", "gx", None),
            P(("member", "gx"), None),
            P(None, "gx", None),
            P(None, "gx", None),
            P("gx", None),
            P(),
            P(),
            P(),
        ),
        out_specs=(P("member", "gx", None), P(("member", "gx"), None), P("member", "gx")),
        check_vma=False,
    )
```

```python
import functools

import jax
import jax.numpy as jnp
from jax import lax
from jax.experimental import pallas as pl
from jax.experimental.pallas import tpu as pltpu
from jax.sharding import PartitionSpec as P

ITERS = 4
SEG = 8
GMAX = 0.3

CENTER = 4.5
HALF = 4.5
CANCEL = 2000.0

LANES = 128
SUB = 8
PAD = 16
LSLOT = 16

f32 = jnp.float32


def edge_rows(cells, width):
    count = lax.axis_size("gx")
    below = lax.ppermute(cells[-width:], "gx", [(i, i + 1) for i in range(count - 1)])
    above = lax.ppermute(cells[:width], "gx", [(i + 1, i) for i in range(count - 1)])
    return below, above


def apply_surface(field, surface_coef):
    before, after = edge_rows(field, 1)
    padded = jnp.concatenate([before, field, after], axis=0)
    padded = jnp.pad(padded, ((0, 0), (1, 1)))
    beside = padded[2:, 1:-1] + padded[:-2, 1:-1] + padded[1:-1, 2:] + padded[1:-1, :-2]
    return (4.0 + surface_coef) * field - beside


def squares_sum(residue):
    return lax.psum(jnp.sum(residue * residue), "gx")


def plain_solve(adj_eta, surface_coef):
    adj_free = jnp.zeros_like(adj_eta)
    residue = adj_eta
    search = adj_eta
    norm_now = squares_sum(residue)
    for _ in range(ITERS):
        image = apply_surface(search, surface_coef)
        alpha = norm_now / lax.psum(jnp.sum(search * image), "gx")
        adj_free = adj_free + alpha * search
        residue = residue - alpha * image
        norm_next = squares_sum(residue)
        search = residue + norm_next / norm_now * search
        norm_now = norm_next
    before, after = edge_rows(adj_free, 1)
    blank = jnp.zeros((SUB - 1, adj_eta.shape[1]), f32)
    return adj_free, jnp.concatenate([blank, before, after, blank], axis=0)


def beside_tiles(tiles, lane):
    to_east = [pltpu.roll(t, 1, 1) for t in tiles]
    to_west = [pltpu.roll(t, LANES - 1, 1) for t in tiles]
    zero = jnp.zeros_like(tiles[0])
    west = [
        jnp.where(lane == 0, to_east[c - 1] if c else zero, to_east[c]) for c in range(len(tiles))
    ]
    east = [
        jnp.where(lane == LANES - 1, to_west[c + 1] if c + 1 < len(tiles) else zero, to_west[c])
        for c in range(len(tiles))
    ]
    return west, east


def tiles_of(ref, lead, row, count):
    return [ref[(*lead, pl.ds(row, SUB), pl.ds(LANES * c, LANES))] for c in range(count)]


def next_tiles(here, north, south, scale, before, lane):
    west, east = beside_tiles(here, lane)
    out = []
    for c in range(len(here)):
        ring = (north[c] + south[c]) + (west[c] + east[c])
        image = scale[c] * here[c] - (1.0 / HALF) * ring
        out.append(image if before is None else 2.0 * image - before[c])
    return out


def products(here, after):
    return (
        functools.reduce(jnp.add, [a * a for a in here]),
        functools.reduce(jnp.add, [a * b for a, b in zip(here, after, strict=True)]),
    )


def centred(coef):
    return (coef - (CENTER - 4.0)) * (1.0 / HALF)


def inner_basis(eta, coef, inner, partial, diag):
    rows, cols = eta.shape
    wide = cols // LANES
    lane = lax.broadcasted_iota(jnp.int32, (SUB, LANES), 1)
    inner[0, SUB : SUB + rows, :] = eta[...]
    diag[...] = centred(coef[...])
    for k in range(ITERS):
        inner[k, 0:SUB, :] = jnp.zeros((SUB, cols), f32)
        inner[k, SUB + rows : 2 * SUB + rows, :] = jnp.zeros((SUB, cols), f32)
    totals = [jnp.zeros((SUB, LANES), f32) for _ in range(2 * ITERS)]
    for k in range(ITERS):
        last = k == ITERS - 1
        for start in range(SUB, rows, SUB) if last else range(0, rows, SUB):
            counted = SUB <= start < rows - SUB
            if last and not counted:
                continue
            here = tiles_of(inner, (k,), SUB + start, wide)
            north = tiles_of(inner, (k,), SUB + start - 1, wide)
            south = tiles_of(inner, (k,), SUB + start + 1, wide)
            before = tiles_of(inner, (k - 1,), SUB + start, wide) if k else None
            after = next_tiles(here, north, south, tiles_of(diag, (), start, wide), before, lane)
            if not last:
                for c in range(wide):
                    inner[k + 1, pl.ds(SUB + start, SUB), pl.ds(LANES * c, LANES)] = after[c]
            if counted:
                even_sum, odd_sum = products(here, after)
                totals[2 * k] += even_sum
                totals[2 * k + 1] += odd_sum
    for i, total in enumerate(totals):
        partial[i] = total


def outer_kernel(eta, coef, inner, partial, first, second, edge, sums, diag):
    me = lax.axis_index("gx")
    count = lax.axis_size("gx")
    rows, cols = eta.shape
    wide = cols // LANES
    even = lax.rem(me, 2) == 0
    lane = lax.broadcasted_iota(jnp.int32, (SUB, LANES), 1)
    totals = [partial[i] for i in range(2 * ITERS)]
    zeros = jnp.zeros((SUB, cols), f32)
    up = jnp.where(even, second[...], first[...])
    down = jnp.where(even, first[...], second[...])
    for side in range(2):
        own = 2 * SUB if side == 0 else SUB
        beyond = SUB if side == 0 else 2 * SUB
        outside = 0 if side == 0 else 3 * SUB
        beside = 3 * SUB if side == 0 else 0
        line = 0 if side == 0 else rows - SUB
        beside_line = SUB if side == 0 else rows - 2 * SUB
        got = up if side == 0 else down
        exists = jnp.where((me > 0) if side == 0 else (me < count - 1), 1.0, 0.0).astype(f32)
        for k in range(ITERS):
            edge[k, side, pl.ds(outside, SUB), :] = zeros
            edge[k, side, pl.ds(beside, SUB), :] = inner[k, pl.ds(SUB + beside_line, SUB), :]
        blank = jnp.zeros((SUB - ITERS, cols), f32)
        if side == 0:
            eta_got = jnp.concatenate([blank, got[:ITERS]], axis=0)
            coef_got = jnp.concatenate([blank, got[ITERS:]], axis=0)
        else:
            eta_got = jnp.concatenate([got[:ITERS], blank], axis=0)
            coef_got = jnp.concatenate([got[ITERS:], blank], axis=0)
        edge[0, side, pl.ds(beyond, SUB), :] = eta_got
        edge[0, side, pl.ds(own, SUB), :] = eta[pl.ds(line, SUB), :]
        diag[side, pl.ds(beyond, SUB), :] = centred(coef_got)
        diag[side, pl.ds(own, SUB), :] = centred(coef[pl.ds(line, SUB), :])
        for k in range(ITERS):
            last = k == ITERS - 1
            for start in (own,) if last else (own, beyond):
                here = tiles_of(edge, (k, side), start, wide)
                north = tiles_of(edge, (k, side), start - 1, wide)
                south = tiles_of(edge, (k, side), start + 1, wide)
                before = tiles_of(edge, (k - 1, side), start, wide) if k else None
                scale = tiles_of(diag, (side,), start, wide)
                after = next_tiles(here, north, south, scale, before, lane)
                if start == beyond:
                    after = [a * exists for a in after]
                if not last:
                    for c in range(wide):
                        at = (pl.ds(start, SUB), pl.ds(LANES * c, LANES))
                        edge[(k + 1, side, *at)] = after[c]
                if start == own:
                    even_sum, odd_sum = products(here, after)
                    totals[2 * k] += even_sum
                    totals[2 * k + 1] += odd_sum
    packed = jnp.concatenate([jnp.sum(t, axis=0, keepdims=True) for t in totals], axis=0)
    for to in range(sums.shape[0]):
        sums[to] = packed


def solve_coefficients(moments):
    scaled = [m / moments[0] for m in moments]
    mu = scaled[:2] + [2.0 * scaled[i] - scaled[i % 2] for i in range(2, 2 * ITERS)]

    def gram(i, j):
        if i == j or abs(i - j) == 1:
            return scaled[i + j]
        return 0.5 * (mu[i + j] + mu[abs(i - j)])

    def image_of(p):
        out = [CENTER * a for a in p] + [None]

        def add(i, v):
            out[i] = v if out[i] is None else out[i] + v

        for i, a in enumerate(p):
            if i == 0:
                add(1, HALF * a)
            else:
                add(i + 1, (0.5 * HALF) * a)
                add(i - 1, (0.5 * HALF) * a)
        return out

    def product(p, q):
        terms = [a * b * gram(i, j) for i, a in enumerate(p) for j, b in enumerate(q)]
        return functools.reduce(jnp.add, terms), functools.reduce(jnp.add, map(jnp.abs, terms))

    def plus(p, scale, q):
        out = []
        for i in range(max(len(p), len(q))):
            if i >= len(q):
                out.append(p[i])
            elif i >= len(p):
                out.append(scale * q[i])
            else:
                out.append(p[i] + scale * q[i])
        return out

    one = jnp.ones_like(moments[0])
    solved, residue, search, norm_now = [], [one], [one], one
    sound = jnp.isfinite(moments[0]) & (moments[0] > 0.0)
    for step in range(ITERS):
        image = image_of(search)
        value, size = product(search, image)
        sound = sound & (size < CANCEL * value)
        alpha = norm_now / value
        solved = plus(solved, alpha, search)
        if step < ITERS - 1:
            residue = plus(residue, -alpha, image)
            norm_next, size = product(residue, residue)
            sound = sound & (size < CANCEL * norm_next)
            search = plus(residue, norm_next / norm_now, search)
            norm_now = norm_next
    return solved, sound


def rate(dist, widths, side):
    width = widths[side]
    ramp = jnp.maximum(width - dist, 0).astype(f32)
    return ramp * GMAX / jnp.broadcast_to(width.astype(f32), dist.shape)


def tile_iotas():
    lane = lax.broadcasted_iota(jnp.int32, (SUB, LANES), 1)
    sub = lax.broadcasted_iota(jnp.int32, (SUB, LANES), 0)
    return lane, sub


def side_rates(widths, me, count, rows):
    lane, sub = tile_iotas()
    return (
        rate(lane, widths, 0),
        rate(LANES - 1 - lane, widths, 1),
        rate(me * rows + sub, widths, 2),
        rate((count - 1 - me) * rows + (SUB - 1) - sub, widths, 3),
    )


def ready_kernel(
    thickness, widths, eta, coef, theta2, diffusivity, mask,
    inner, partial, near, far, end_part, end_weight,
    diag, theta_ends, mask_ends, spread_ends, sems,
):
    levels, rows, cols = theta2.shape
    me = lax.axis_index("gx")
    count = lax.axis_size("gx")
    even = lax.rem(me, 2) == 0
    wide = cols // LANES
    half = spread_ends.shape[2]
    copies = []
    for e in range(2):
        ends = pl.ds(0 if e == 0 else rows - SUB, SUB)
        thick = pl.ds(0 if e == 0 else rows - half, half)
        copies += [
            pltpu.make_async_copy(theta2.at[:, ends, :], theta_ends.at[e], sems.at[3 * e]),
            pltpu.make_async_copy(mask.at[:, ends, :], mask_ends.at[e], sems.at[3 * e + 1]),
            pltpu.make_async_copy(diffusivity.at[:, thick, :], spread_ends.at[e], sems.at[3 * e + 2]),
        ]
    for copy in copies:
        copy.start()
    inner_basis(eta, coef, inner, partial, diag)
    for copy in copies:
        copy.wait()

    _, sub = tile_iotas()
    rates = side_rates(widths, me, count, rows)
    for l in range(levels):
        rows_of = []
        for e in range(2):
            line = 0 if e == 0 else SUB - 1
            deep = 0 if e == 0 else half - 1
            wet = mask_ends[e, l, line : line + 1, :] != 0
            spread = spread_ends[e, l, :, :].astype(f32)[deep : deep + 1, :]
            root = jnp.where(wet, spread * lax.rsqrt(spread), 0.0)
            rows_of.append((theta_ends[e, l, line : line + 1, :], root))
        for i in range(2):
            near[levels * i + l : levels * i + l + 1, :] = jnp.where(even, rows_of[1][i], rows_of[0][i])
            far[levels * i + l : levels * i + l + 1, :] = jnp.where(even, rows_of[0][i], rows_of[1][i])

    def end(e):
        for c in range(wide):
            cut = pl.ds(LANES * c, LANES)
            for low in range(0, LSLOT, SUB):
                kept = jnp.zeros((SUB, LANES), f32)
                for l in range(low, min(low + SUB, levels)):
                    wet_rate = jnp.where(mask_ends[e, l, :, cut] != 0, rates[2 + e], 0.0)
                    part = jnp.sum(theta_ends[e, l, :, cut] * wet_rate, axis=0, keepdims=True)
                    kept = jnp.where(sub + low == l, part, kept)
                    end_weight[e, l, :, cut] = thickness[l] * wet_rate
                end_part[e, pl.ds(low, SUB), cut] = kept

    @pl.when(me == 0)
    def _():
        end(0)

    @pl.when(me == count - 1)
    def _():
        end(1)


def sides_kernel(thickness, widths, _after, theta2, mask, part, weight, theta_sides, mask_sides, sems):
    levels, rows, cols = theta2.shape
    me = lax.axis_index("gx")
    count = lax.axis_size("gx")
    copies = []
    for e in range(2):
        lanes = pl.ds(0 if e == 0 else cols - LANES, LANES)
        copies += [
            pltpu.make_async_copy(theta2.at[:, :, lanes], theta_sides.at[e], sems.at[2 * e]),
            pltpu.make_async_copy(mask.at[:, :, lanes], mask_sides.at[e], sems.at[2 * e + 1]),
        ]
    for copy in copies:
        copy.start()
    for copy in copies:
        copy.wait()
    lane, sub = tile_iotas()
    rates = side_rates(widths, me, count, rows)
    for side in range(2):
        for start in range(0, rows, SUB):
            kept = jnp.zeros((SUB, LANES), f32)
            for l in range(levels):
                at = (side, l, pl.ds(start, SUB), slice(None))
                wet_rate = jnp.where(mask_sides[at] != 0, rates[side], 0.0)
                total = jnp.sum(theta_sides[at] * wet_rate, axis=1, keepdims=True)
                kept = jnp.where(lane == sub * LSLOT + l, total, kept)
                weight[at] = thickness[l] * wet_rate
            part[side, pl.ds(start, SUB), :] = kept


def fill_sent(slot_of, field, end_part, end_weight, side_part, side_weight, sent, ends, lines):
    rows, cols = field.shape
    levels = side_weight.shape[1]
    me = lax.axis_index("gx")
    count = lax.axis_size("gx")
    total_rows = rows * count
    lane, sub = tile_iotas()
    sent[...] = jnp.zeros(sent.shape, f32)
    own = rows // SEG
    for side in range(2):
        cut = pl.ds(0 if side == 0 else cols - LANES, LANES)
        for s in range(own):
            at = pl.ds(SUB * s, SUB)
            free = field[at, cut]
            kept = jnp.zeros((SUB, LANES), f32)
            for l in range(levels):
                part = jnp.sum(side_weight[side, l, at, :] * free, axis=1, keepdims=True)
                kept = jnp.where(lane == sub * LSLOT + l, part, kept)
            row = jnp.sum(kept + side_part[side, at, :], axis=0, keepdims=True)
            slot = slot_of[side * (total_rows // SEG) + me * own + s]
            sent[pl.ds(slot, 1), :] = row
    across = cols // SEG

    def end_rows(e):
        for c in range(cols // LANES):
            cut = pl.ds(LANES * c, LANES)
            free = field[pl.ds(0 if e == 0 else rows - SUB, SUB), cut]
            for low in range(0, LSLOT, SUB):
                kept = end_part[e, pl.ds(low, SUB), cut]
                for l in range(low, min(low + SUB, levels)):
                    part = jnp.sum(end_weight[e, l, :, cut] * free, axis=0, keepdims=True)
                    kept = jnp.where(sub + low == l, kept + part, kept)
                ends[pl.ds(low, SUB), cut] = kept
        values = ends[...]
        phase = lax.rem(lax.broadcasted_iota(jnp.int32, values.shape, 1), SEG)
        stacked = jnp.concatenate([jnp.where(phase == r, values, 0.0) for r in range(SEG)], axis=0)
        pick = (
            lax.broadcasted_iota(jnp.int32, (across, cols), 1) // SEG
            == lax.broadcasted_iota(jnp.int32, (across, cols), 0)
        ).astype(f32)
        lines[...] = lax.dot_general(
            pick, stacked, (((1,), (1,)), ((), ())),
            precision=lax.Precision.HIGHEST, preferred_element_type=f32,
        )
        base = 2 * (total_rows // SEG) + e * across

        @pl.loop(0, across)
        def _(s):
            sent[pl.ds(slot_of[base + s], 1), :] = lines[pl.ds(s, 1), :]

    @pl.when(me == 0)
    def _():
        end_rows(0)

    @pl.when(me == count - 1)
    def _():
        end_rows(1)


def field_kernel(
    slot_of, sums, inner, edge, end_part, end_weight, side_part, side_weight,
    field, halo, sent, sound_out, ends, lines,
):
    count = sums.shape[0]
    rows, cols = field.shape
    total = sums[0]
    for source in range(1, count):
        total = total + sums[source]
    across = jnp.sum(total, axis=1, keepdims=True)
    moments = [jnp.broadcast_to(across[m : m + 1, :], (SUB, LANES)) for m in range(2 * ITERS)]
    solved, sound = solve_coefficients(moments)
    sound_out[0] = jnp.min(jnp.where(sound, 1, 0))

    def mixed(parts):
        return functools.reduce(jnp.add, [a * p for a, p in zip(solved, parts, strict=True)])

    for c in range(cols // LANES):
        cut = pl.ds(LANES * c, LANES)

        def at_edge(side, row):
            return mixed([edge[k, side, pl.ds(row, SUB), cut] for k in range(ITERS)])

        halo[0:SUB, cut] = at_edge(0, SUB)
        field[0:SUB, cut] = at_edge(0, 2 * SUB)
        field[rows - SUB : rows, cut] = at_edge(1, SUB)
        halo[SUB : 2 * SUB, cut] = at_edge(1, 2 * SUB)
        for start in range(SUB, rows - SUB, SUB):
            at = pl.ds(SUB + start, SUB)
            field[pl.ds(start, SUB), cut] = mixed([inner[k, at, cut] for k in range(ITERS)])
    fill_sent(slot_of, field, end_part, end_weight, side_part, side_weight, sent, ends, lines)


def tracer_kernel(
    thickness, widths, field, halo, near, far, theta2, diffusivity, mask,
    out, theta_all, spread_all, mask_all, scaled, roots, beyond, in_sems, out_sems,
):
    me = lax.axis_index("gx")
    count = lax.axis_size("gx")
    levels, rows, cols = theta2.shape
    wide = cols // LANES
    even = lax.rem(me, 2) == 0
    lane, _ = tile_iotas()
    west_rate, east_rate, south_rate, north_rate = side_rates(widths, me, count, rows)

    def loads(l):
        pairs = ((theta2, theta_all), (diffusivity, spread_all), (mask, mask_all))
        return [
            pltpu.make_async_copy(a.at[l], b.at[l], in_sems.at[i, l])
            for i, (a, b) in enumerate(pairs)
        ]

    def store(l):
        return pltpu.make_async_copy(theta_all.at[l], out.at[l], out_sems.at[l])

    for l in range(levels):
        for copy in loads(l):
            copy.start()

    for side in range(2):
        mine, other = (far, near) if side == 0 else (near, far)
        theta_row = jnp.where(even, mine[0:levels, :], other[0:levels, :])
        root_row = jnp.where(even, mine[levels : 2 * levels, :], other[levels : 2 * levels, :])
        line = SUB - 1 if side == 0 else SUB
        free = halo[line : line + 1, :]
        deep = jnp.concatenate([thickness[l] * free for l in range(levels)], axis=0)
        total = theta_row + jnp.where(root_row > 0.0, deep, 0.0)
        line_lane = lax.broadcasted_iota(jnp.int32, (levels, cols), 1)
        gamma = rate(line_lane, widths, 0) + rate(cols - 1 - line_lane, widths, 1)
        lines = root_row * ((1.0 - gamma) * total)
        for l in range(levels):
            beyond[side, l] = lines[l : l + 1, :]

    @pl.loop(0, levels)
    def _(level):
        for copy in loads(level):
            copy.wait()
        scaled[SUB - 1 : SUB, :] = beyond[0, level]
        scaled[SUB + rows : SUB + rows + 1, :] = beyond[1, level]
        weight = thickness[level]
        for start in range(0, rows, SUB):
            for c in range(wide):
                at = (pl.ds(start, SUB), pl.ds(LANES * c, LANES))
                wet = mask_all[(level, *at)] != 0
                total = theta_all[(level, *at)] + jnp.where(wet, weight * field[at], 0.0)
                parts = [
                    r
                    for r, there in (
                        (west_rate, c == 0),
                        (east_rate, c == wide - 1),
                        (south_rate, start == 0),
                        (north_rate, start == rows - SUB),
                    )
                    if there
                ]
                one = total
                if parts:
                    one = jnp.where(wet, 1.0 - functools.reduce(jnp.add, parts), 1.0) * total
                spread = spread_all[(level, *at)].astype(f32)
                root = jnp.where(wet, spread * lax.rsqrt(spread), 0.0)
                theta_all[(level, *at)] = one
                roots[at] = root
                scaled[pl.ds(SUB + start, SUB), pl.ds(LANES * c, LANES)] = root * one
        for start in range(0, rows, SUB):
            here = tiles_of(scaled, (), SUB + start, wide)
            north = tiles_of(scaled, (), SUB + start - 1, wide)
            south = tiles_of(scaled, (), SUB + start + 1, wide)
            west, east = beside_tiles(here, lane)
            for c in range(wide):
                at = (pl.ds(start, SUB), pl.ds(LANES * c, LANES))
                ring = (north[c] + south[c]) + (west[c] + east[c])
                theta_all[(level, *at)] += roots[at] * (ring - 4.0 * here[c])
        store(level).start()

    for l in range(levels):
        store(l).wait()


def rim_kernel(got, rim):
    count, height, _ = got.shape
    levels, width = rim.shape
    total = got[0]
    for source in range(1, count):
        total = total + got[source]
    square = jnp.concatenate([total, jnp.zeros((LANES - height, LANES), f32)], axis=0)
    turned = square.T
    spread = (
        lax.broadcasted_iota(jnp.int32, (LANES, width), 1) // SEG
        == lax.broadcasted_iota(jnp.int32, (LANES, width), 0)
    ).astype(f32)
    wide = jnp.dot(turned, spread, precision=lax.Precision.HIGHEST, preferred_element_type=f32)
    phase = lax.rem(lax.broadcasted_iota(jnp.int32, (LSLOT, width), 1), SEG)
    lines = jnp.zeros((LSLOT, width), f32)
    for r in range(SEG):
        lines = lines + jnp.where(phase == r, wide[LSLOT * r : LSLOT * (r + 1), :], 0.0)
    rim[...] = lines[:levels, :]


VMEM = pl.BlockSpec(memory_space=pltpu.VMEM)
SMEM = pl.BlockSpec(memory_space=pltpu.SMEM)
ANY = pl.BlockSpec(memory_space=pl.ANY)


def whole(shape):
    return pl.BlockSpec(shape, lambda *_: (0,) * len(shape))


def local_call(kernel, name, outs, ins, out_specs=None, scratch=(), limit=32, **more):
    return pl.pallas_call(
        kernel,
        out_shape=tuple(jax.ShapeDtypeStruct(*o) if isinstance(o, tuple) else o for o in outs),
        in_specs=ins,
        out_specs=out_specs or tuple(VMEM for _ in outs),
        scratch_shapes=list(scratch),
        compiler_params=pltpu.CompilerParams(vmem_limit_bytes=limit * 2**20),
        name=name,
        **more,
    )


def shards(
    adj_theta2, adj_eta, diffusivity, land_mask, surface_coef, thickness, seg_perm, sponge_width
):
    levels, rows, cols = adj_theta2.shape
    count = lax.axis_size("gx")
    me = lax.axis_index("gx")
    even = lax.rem(me, 2) == 0
    local_segs = (2 * rows * count + 2 * cols) // SEG // count
    slots = -(-local_segs // SUB) * SUB
    slot_of = seg_perm // local_segs * slots + seg_perm % local_segs
    inner_pairs = [(i, i ^ 1) for i in range(count)]
    outer_pairs = [p for i in range(1, count - 1, 2) for p in ((i, i + 1), (i + 1, i))]

    def edges(at_end):
        start = jnp.where(at_end, rows - ITERS, 0)
        return jnp.concatenate(
            [lax.dynamic_slice_in_dim(a, start, ITERS, 0) for a in (adj_eta, surface_coef)]
        )

    fields = [
        pltpu.with_memory_space_constraint(a, pltpu.HBM)
        for a in (adj_theta2, diffusivity, land_mask)
    ]
    first = lax.ppermute(edges(even), "gx", inner_pairs)
    second = lax.ppermute(edges(jnp.logical_not(even)), "gx", outer_pairs)

    inner, partial, near, far, *ends = local_call(
        ready_kernel,
        "ready",
        [
            ((ITERS, rows + 2 * SUB, cols), f32),
            ((2 * ITERS, SUB, LANES), f32),
            ((2 * levels, cols), f32),
            ((2 * levels, cols), f32),
            ((2, LSLOT, cols), f32),
            ((2, levels, SUB, cols), f32),
        ],
        [SMEM, SMEM, VMEM, VMEM, ANY, ANY, ANY],
        scratch=[
            pltpu.VMEM((rows, cols), f32),
            pltpu.VMEM((2, levels, SUB, cols), f32),
            pltpu.VMEM((2, levels, SUB, cols), jnp.int32),
            pltpu.VMEM((2, levels, 2 * SUB, cols), diffusivity.dtype),
            pltpu.SemaphoreType.DMA((6,)),
        ],
        cost_estimate=pl.CostEstimate(flops=10**6, bytes_accessed=4 * 10**6, transcendentals=0),
    )(thickness, sponge_width, adj_eta, surface_coef, *fields)
    edge, sums = local_call(
        outer_kernel,
        "outer",
        [((ITERS, 2, 4 * SUB, cols), f32), ((count, 2 * ITERS, LANES), f32)],
        [VMEM] * 6,
        scratch=[pltpu.VMEM((2, 4 * SUB, cols), f32)],
    )(adj_eta, surface_coef, inner, partial, first, second)
    sums, near, far = lax.optimization_barrier((sums, near, far))
    all_sums = lax.all_to_all(sums, "gx", 0, 0)
    near = lax.ppermute(near, "gx", inner_pairs)
    far = lax.ppermute(far, "gx", outer_pairs)

    sent_shape = ((count * slots, LANES), f32)
    sent_scratch = [pltpu.VMEM((LSLOT, cols), f32), pltpu.VMEM((cols // SEG, LANES), f32)]
    sides = local_call(
        sides_kernel,
        "sides",
        [((2, rows, LANES), f32), ((2, levels, rows, LANES), f32)],
        [SMEM, SMEM, ANY, ANY, ANY],
        scratch=[
            pltpu.VMEM((2, levels, rows, LANES), f32),
            pltpu.VMEM((2, levels, rows, LANES), jnp.int32),
            pltpu.SemaphoreType.DMA((4,)),
        ],
        cost_estimate=pl.CostEstimate(flops=10**6, bytes_accessed=2 * 10**6, transcendentals=0),
    )(thickness, sponge_width, sums, fields[0], fields[2])
    field, halo, sent, sound = local_call(
        field_kernel,
        "field",
        [((rows, cols), f32), ((2 * SUB, cols), f32), sent_shape, ((1,), jnp.int32)],
        [SMEM] + [VMEM] * 7,
        out_specs=(VMEM, VMEM, VMEM, SMEM),
        scratch=sent_scratch,
    )(slot_of, all_sums, inner, edge, *ends, *sides)

    def route(rows_out):
        got = lax.all_to_all(rows_out.reshape(count, slots, LANES), "gx", 0, 0)
        (adj_rim,) = local_call(
            rim_kernel, "rim", [((levels, local_segs * SEG), f32)], [VMEM]
        )(got)
        return adj_rim

    def tracer(free, beyond):
        (adj_theta,) = local_call(
            tracer_kernel,
            "tracer",
            [((levels, rows, cols), f32)],
            [SMEM] * 2 + [VMEM] * 4 + [ANY] * 3,
            out_specs=(ANY,),
            scratch=[
                pltpu.VMEM((levels, rows, cols), f32),
                pltpu.VMEM((levels, rows, cols), diffusivity.dtype),
                pltpu.VMEM((levels, rows, cols), jnp.int32),
                pltpu.VMEM((rows + 2 * SUB, cols), f32),
                pltpu.VMEM((rows, cols), f32),
                pltpu.VMEM((2, levels, 1, cols), f32),
                pltpu.SemaphoreType.DMA((3, levels)),
                pltpu.SemaphoreType.DMA((levels,)),
            ],
            limit=16,
            cost_estimate=pl.CostEstimate(
                flops=24 * 10**6, bytes_accessed=12 * 10**6, transcendentals=10**6
            ),
        )(
            thickness, sponge_width, free, beyond, near, far, *fields
        )
        return adj_theta

    sent, near, far = lax.optimization_barrier((sent, near, far))
    adj_rim = route(sent)
    adj_theta = tracer(field, halo)

    def again():
        free, beyond = plain_solve(adj_eta, surface_coef)
        (rows_out,) = local_call(
            fill_sent, "refill", [sent_shape], [SMEM] + [VMEM] * 5, scratch=sent_scratch
        )(slot_of, free, *ends, *sides)
        return tracer(free, beyond), free, route(rows_out)

    return lax.cond(sound[0] > 0, lambda: (adj_theta, field, adj_rim), again)


def solution(mesh):
    return jax.shard_map(
        shards,
        mesh=mesh,
        in_specs=(
            P("member", "gx", None),
            P(("member", "gx"), None),
            P(None, "gx", None),
            P(None, "gx", None),
            P("gx", None),
            P(),
            P(),
            P(),
        ),
        out_specs=(P("member", "gx", None), P(("member", "gx"), None), P("member", "gx")),
        check_vma=False,
    )
```

```python
import functools

import jax
import jax.numpy as jnp
from jax import lax
from jax.experimental import pallas as pl
from jax.experimental.pallas import tpu as pltpu
from jax.sharding import PartitionSpec as P

ITERS = 4
SEG = 8
GMAX = 0.3

CENTER = 4.5
HALF = 4.5
CANCEL = 2000.0

LANES = 128
SUB = 8
PAD = 16

f32 = jnp.float32


def edge_rows(cells, width):
    count = lax.axis_size("gx")
    below = lax.ppermute(cells[-width:], "gx", [(i, i + 1) for i in range(count - 1)])
    above = lax.ppermute(cells[:width], "gx", [(i + 1, i) for i in range(count - 1)])
    return below, above


def apply_surface(field, surface_coef):
    before, after = edge_rows(field, 1)
    padded = jnp.concatenate([before, field, after], axis=0)
    padded = jnp.pad(padded, ((0, 0), (1, 1)))
    beside = padded[2:, 1:-1] + padded[:-2, 1:-1] + padded[1:-1, 2:] + padded[1:-1, :-2]
    return (4.0 + surface_coef) * field - beside


def squares_sum(residue):
    return lax.psum(jnp.sum(residue * residue), "gx")


def plain_solve(adj_eta, surface_coef):
    adj_free = jnp.zeros_like(adj_eta)
    residue = adj_eta
    search = adj_eta
    norm_now = squares_sum(residue)
    for _ in range(ITERS):
        image = apply_surface(search, surface_coef)
        alpha = norm_now / lax.psum(jnp.sum(search * image), "gx")
        adj_free = adj_free + alpha * search
        residue = residue - alpha * image
        norm_next = squares_sum(residue)
        search = residue + norm_next / norm_now * search
        norm_now = norm_next
    before, after = edge_rows(adj_free, 1)
    blank = jnp.zeros((SUB - 1, adj_eta.shape[1]), f32)
    return adj_free, jnp.concatenate([blank, before, after, blank], axis=0)


def beside_tiles(tiles, lane):
    to_east = [pltpu.roll(t, 1, 1) for t in tiles]
    to_west = [pltpu.roll(t, LANES - 1, 1) for t in tiles]
    zero = jnp.zeros_like(tiles[0])
    west = [
        jnp.where(lane == 0, to_east[c - 1] if c else zero, to_east[c]) for c in range(len(tiles))
    ]
    east = [
        jnp.where(lane == LANES - 1, to_west[c + 1] if c + 1 < len(tiles) else zero, to_west[c])
        for c in range(len(tiles))
    ]
    return west, east


def tiles_of(ref, lead, row, count):
    return [ref[(*lead, pl.ds(row, SUB), pl.ds(LANES * c, LANES))] for c in range(count)]


def next_tiles(here, north, south, scale, before, lane):
    west, east = beside_tiles(here, lane)
    out = []
    for c in range(len(here)):
        ring = (north[c] + south[c]) + (west[c] + east[c])
        image = scale[c] * here[c] - (1.0 / HALF) * ring
        out.append(image if before is None else 2.0 * image - before[c])
    return out


def products(here, after):
    return (
        functools.reduce(jnp.add, [a * a for a in here]),
        functools.reduce(jnp.add, [a * b for a, b in zip(here, after, strict=True)]),
    )


def centred(coef):
    return (coef - (CENTER - 4.0)) * (1.0 / HALF)


def inner_basis(inner, partial, diag):
    rows, cols = diag.shape
    wide = cols // LANES
    lane = lax.broadcasted_iota(jnp.int32, (SUB, LANES), 1)
    diag[...] = centred(diag[...])
    for k in range(ITERS):
        inner[k, 0:SUB, :] = jnp.zeros((SUB, cols), f32)
        inner[k, SUB + rows : 2 * SUB + rows, :] = jnp.zeros((SUB, cols), f32)
    totals = [jnp.zeros((SUB, LANES), f32) for _ in range(2 * ITERS)]
    for k in range(ITERS):
        last = k == ITERS - 1
        for start in range(SUB, rows, SUB) if last else range(0, rows, SUB):
            counted = SUB <= start < rows - SUB
            if last and not counted:
                continue
            here = tiles_of(inner, (k,), SUB + start, wide)
            north = tiles_of(inner, (k,), SUB + start - 1, wide)
            south = tiles_of(inner, (k,), SUB + start + 1, wide)
            before = tiles_of(inner, (k - 1,), SUB + start, wide) if k else None
            after = next_tiles(here, north, south, tiles_of(diag, (), start, wide), before, lane)
            if not last:
                for c in range(wide):
                    inner[k + 1, pl.ds(SUB + start, SUB), pl.ds(LANES * c, LANES)] = after[c]
            if counted:
                even_sum, odd_sum = products(here, after)
                totals[2 * k] += even_sum
                totals[2 * k + 1] += odd_sum
    for i, total in enumerate(totals):
        partial[i] = total


def outer_kernel(inner, diag, partial, first, second, kept, sums, edge, scale_of):
    me = lax.axis_index("gx")
    count = lax.axis_size("gx")
    rows, cols = diag.shape
    wide = cols // LANES
    even = lax.rem(me, 2) == 0
    lane = lax.broadcasted_iota(jnp.int32, (SUB, LANES), 1)
    totals = [partial[i] for i in range(2 * ITERS)]
    zeros = jnp.zeros((SUB, cols), f32)
    up = jnp.where(even, second[...], first[...])
    down = jnp.where(even, first[...], second[...])
    for side in range(2):
        own = 2 * SUB if side == 0 else SUB
        beyond = SUB if side == 0 else 2 * SUB
        outside = 0 if side == 0 else 3 * SUB
        beside = 3 * SUB if side == 0 else 0
        line = 0 if side == 0 else rows - SUB
        beside_line = SUB if side == 0 else rows - 2 * SUB
        got = up if side == 0 else down
        exists = jnp.where((me > 0) if side == 0 else (me < count - 1), 1.0, 0.0).astype(f32)
        for k in range(ITERS):
            edge[k, side, pl.ds(outside, SUB), :] = zeros
            edge[k, side, pl.ds(beside, SUB), :] = inner[k, pl.ds(SUB + beside_line, SUB), :]
        blank = jnp.zeros((SUB - ITERS, cols), f32)
        if side == 0:
            eta_got = jnp.concatenate([blank, got[:ITERS]], axis=0)
            coef_got = jnp.concatenate([blank, got[ITERS:]], axis=0)
        else:
            eta_got = jnp.concatenate([got[:ITERS], blank], axis=0)
            coef_got = jnp.concatenate([got[ITERS:], blank], axis=0)
        edge[0, side, pl.ds(beyond, SUB), :] = eta_got
        edge[0, side, pl.ds(own, SUB), :] = inner[0, pl.ds(SUB + line, SUB), :]
        scale_of[side, pl.ds(beyond, SUB), :] = centred(coef_got)
        scale_of[side, pl.ds(own, SUB), :] = diag[pl.ds(line, SUB), :]
        for k in range(ITERS):
            last = k == ITERS - 1
            for start in (own,) if last else (own, beyond):
                here = tiles_of(edge, (k, side), start, wide)
                north = tiles_of(edge, (k, side), start - 1, wide)
                south = tiles_of(edge, (k, side), start + 1, wide)
                before = tiles_of(edge, (k - 1, side), start, wide) if k else None
                scale = tiles_of(scale_of, (side,), start, wide)
                after = next_tiles(here, north, south, scale, before, lane)
                if start == beyond:
                    after = [a * exists for a in after]
                if not last:
                    for c in range(wide):
                        at = (pl.ds(start, SUB), pl.ds(LANES * c, LANES))
                        edge[(k + 1, side, *at)] = after[c]
                if start == own:
                    even_sum, odd_sum = products(here, after)
                    totals[2 * k] += even_sum
                    totals[2 * k + 1] += odd_sum
    kept[...] = edge[:, :, SUB : 3 * SUB, :]
    packed = jnp.concatenate([jnp.sum(t, axis=0, keepdims=True) for t in totals], axis=0)
    for to in range(sums.shape[0]):
        sums[to] = packed


def solve_coefficients(moments):
    scaled = [m / moments[0] for m in moments]
    mu = scaled[:2] + [2.0 * scaled[i] - scaled[i % 2] for i in range(2, 2 * ITERS)]

    def gram(i, j):
        if i == j or abs(i - j) == 1:
            return scaled[i + j]
        return 0.5 * (mu[i + j] + mu[abs(i - j)])

    def image_of(p):
        out = [CENTER * a for a in p] + [None]

        def add(i, v):
            out[i] = v if out[i] is None else out[i] + v

        for i, a in enumerate(p):
            if i == 0:
                add(1, HALF * a)
            else:
                add(i + 1, (0.5 * HALF) * a)
                add(i - 1, (0.5 * HALF) * a)
        return out

    def product(p, q):
        terms = [a * b * gram(i, j) for i, a in enumerate(p) for j, b in enumerate(q)]
        return functools.reduce(jnp.add, terms), functools.reduce(jnp.add, map(jnp.abs, terms))

    def plus(p, scale, q):
        out = []
        for i in range(max(len(p), len(q))):
            if i >= len(q):
                out.append(p[i])
            elif i >= len(p):
                out.append(scale * q[i])
            else:
                out.append(p[i] + scale * q[i])
        return out

    one = jnp.ones_like(moments[0])
    solved, residue, search, norm_now = [], [one], [one], one
    sound = jnp.isfinite(moments[0]) & (moments[0] > 0.0)
    for step in range(ITERS):
        image = image_of(search)
        value, size = product(search, image)
        sound = sound & (size < CANCEL * value)
        alpha = norm_now / value
        solved = plus(solved, alpha, search)
        if step < ITERS - 1:
            residue = plus(residue, -alpha, image)
            norm_next, size = product(residue, residue)
            sound = sound & (size < CANCEL * norm_next)
            search = plus(residue, norm_next / norm_now, search)
            norm_now = norm_next
    return solved, sound


def rate(dist, widths, side):
    width = widths[side]
    ramp = jnp.maximum(width - dist, 0).astype(f32)
    return ramp * GMAX / jnp.broadcast_to(width.astype(f32), dist.shape)


def tile_iotas():
    lane = lax.broadcasted_iota(jnp.int32, (SUB, LANES), 1)
    sub = lax.broadcasted_iota(jnp.int32, (SUB, LANES), 0)
    return lane, sub


def side_rates(widths, me, count, rows):
    lane, sub = tile_iotas()
    return (
        rate(lane, widths, 0),
        rate(LANES - 1 - lane, widths, 1),
        rate(me * rows + sub, widths, 2),
        rate((count - 1 - me) * rows + (SUB - 1) - sub, widths, 3),
    )


def ready_kernel(
    thickness, widths, eta, coef, theta2, diffusivity, mask,
    inner, diag, partial, near, far, side_theta, side_weight, end_theta, end_weight,
    theta_ends, mask_ends, spread_ends, theta_sides, mask_sides, end_sems, side_sems, sems,
):
    levels, rows, cols = theta2.shape
    me = lax.axis_index("gx")
    count = lax.axis_size("gx")
    even = lax.rem(me, 2) == 0
    wide = cols // LANES
    half = spread_ends.shape[2]
    end_copies, side_copies = [], []
    for e in range(2):
        ends = pl.ds(0 if e == 0 else rows - SUB, SUB)
        thick = pl.ds(0 if e == 0 else rows - half, half)
        lanes = pl.ds(0 if e == 0 else cols - LANES, LANES)
        end_copies += [
            pltpu.make_async_copy(theta2.at[:, ends, :], theta_ends.at[e], end_sems.at[3 * e]),
            pltpu.make_async_copy(mask.at[:, ends, :], mask_ends.at[e], end_sems.at[3 * e + 1]),
            pltpu.make_async_copy(diffusivity.at[:, thick, :], spread_ends.at[e], end_sems.at[3 * e + 2]),
        ]
        side_copies += [
            pltpu.make_async_copy(theta2.at[:, :, lanes], theta_sides.at[e], side_sems.at[2 * e]),
            pltpu.make_async_copy(mask.at[:, :, lanes], mask_sides.at[e], side_sems.at[2 * e + 1]),
        ]
    rows_copies = [
        pltpu.make_async_copy(eta, inner.at[0, pl.ds(SUB, rows), :], sems.at[0]),
        pltpu.make_async_copy(coef, diag, sems.at[1]),
    ]
    for copy in rows_copies + end_copies + side_copies:
        copy.start()
    for copy in rows_copies:
        copy.wait()
    inner_basis(inner, partial, diag)
    for copy in end_copies:
        copy.wait()

    rates = side_rates(widths, me, count, rows)
    lines = []
    for e in range(2):
        line = 0 if e == 0 else SUB - 1
        deep = 0 if e == 0 else half - 1
        stack = lambda cut: jnp.concatenate([cut(l) for l in range(levels)], axis=0)
        theta = stack(lambda l: theta_ends[e, l, line : line + 1, :])
        wet = stack(lambda l: mask_ends[e, l, line : line + 1, :]) != 0
        spread = stack(lambda l: spread_ends[e, l].astype(f32)[deep : deep + 1, :])
        lines.append((theta, jnp.where(wet, spread * lax.rsqrt(spread), 0.0)))
    for i in range(2):
        at = pl.ds(levels * i, levels)
        near[at, :] = jnp.where(even, lines[1][i], lines[0][i])
        far[at, :] = jnp.where(even, lines[0][i], lines[1][i])

    def end(e):
        for c in range(wide):
            cut = pl.ds(LANES * c, LANES)
            for l in range(levels):
                wet_rate = jnp.where(mask_ends[e, l, :, cut] != 0, rates[2 + e], 0.0)
                part = theta_ends[e, l, :, cut] * wet_rate
                end_theta[l : l + 1, cut] = jnp.sum(part, axis=0, keepdims=True)
                end_weight[l, :, cut] = thickness[l] * wet_rate

    @pl.when(me == 0)
    def _():
        end(0)

    @pl.when(me == count - 1)
    def _():
        end(1)

    for copy in side_copies:
        copy.wait()
    for side in range(2):
        for start in range(0, rows, SUB):
            thetas, weights = [], []
            for l in range(levels):
                at = (side, l, pl.ds(start, SUB), slice(None))
                wet_rate = jnp.where(mask_sides[at] != 0, rates[side], 0.0)
                shift = (SEG * (l + side)) % LANES
                turn = (lambda v: v) if shift == 0 else (lambda v: pltpu.roll(v, shift, 1))
                thetas.append(turn(theta_sides[at] * wet_rate))
                weights.append(turn(thickness[l] * wet_rate))
            side_theta[side, pl.ds(start, SUB), :] = functools.reduce(jnp.add, thetas)
            side_weight[side, pl.ds(start, SUB), :] = functools.reduce(jnp.add, weights)


def exact_dot(few, values, contract):
    out = None
    rest = values
    for _ in range(3):
        part = rest.astype(jnp.bfloat16)
        rest = rest - part.astype(f32)
        pair = (part, few) if contract == "values first" else (few, part)
        dims = (((1,), (0,)), ((), ())) if contract == "values first" else (((1,), (1,)), ((), ()))
        term = lax.dot_general(*pair, dims, preferred_element_type=f32)
        out = term if out is None else out + term
    return out


def fill_sent(slot_of, field, side_theta, side_weight, end_theta, end_weight, sent, lines):
    rows, cols = field.shape
    levels = end_weight.shape[0]
    me = lax.axis_index("gx")
    count = lax.axis_size("gx")
    total_rows = rows * count
    lane, sub = tile_iotas()
    phase = lax.rem(lane, SEG)
    sent[...] = jnp.zeros(sent.shape, f32)
    own = rows // SEG
    for side in range(2):
        cut = pl.ds(0 if side == 0 else cols - LANES, LANES)
        for s in range(own):
            at = pl.ds(SUB * s, SUB)
            free = field[at, cut]
            free = jnp.where(lane < SEG, free if side == 0 else pltpu.roll(free, SEG, 1), 0.0)
            step = SEG
            while step < LANES:
                free = free + pltpu.roll(free, step, 1)
                step *= 2
            cells = side_theta[side, at, :] + side_weight[side, at, :] * free
            for step in (4, 2, 1):
                cells = cells + pltpu.roll(cells, LANES - step, 1)
            cells = pltpu.roll(cells, 0, 1, stride=1, stride_axis=0)
            row = jnp.sum(jnp.where(phase == sub, cells, 0.0), axis=0, keepdims=True)
            slot = slot_of[side * (total_rows // SEG) + me * own + s]
            sent[pl.ds(slot, 1), :] = row
    across = cols // SEG

    def end_rows(e):
        per = LANES // SEG
        pick = (
            lax.broadcasted_iota(jnp.int32, (per, LANES), 1) // SEG
            == lax.broadcasted_iota(jnp.int32, (per, LANES), 0)
        ).astype(jnp.bfloat16)
        for c in range(cols // LANES):
            cut = pl.ds(LANES * c, LANES)
            free = field[pl.ds(0 if e == 0 else rows - SUB, SUB), cut]
            stacked = []
            for l in range(LANES // SUB):
                if l < levels:
                    total = jnp.sum(end_weight[l, :, cut] * free, axis=0, keepdims=True)
                    total = total + end_theta[l : l + 1, cut]
                    stacked.append(jnp.where(phase == sub, total, 0.0))
                else:
                    stacked.append(jnp.zeros((SUB, LANES), f32))
            stacked = jnp.concatenate(stacked, axis=0)
            lines[pl.ds(per * c, per), :] = exact_dot(pick, stacked, "values second")
        base = 2 * (total_rows // SEG) + e * across

        @pl.loop(0, across, unroll=8)
        def _(s):
            sent[pl.ds(slot_of[base + s], 1), :] = lines[pl.ds(s, 1), :]

    @pl.when(me == 0)
    def _():
        end_rows(0)

    @pl.when(me == count - 1)
    def _():
        end_rows(1)


def field_kernel(
    slot_of, sums, inner, edge, side_theta, side_weight, end_theta, end_weight,
    field, halo, sent, sound_out, lines,
):
    count = sums.shape[0]
    rows, cols = field.shape
    total = sums[0]
    for source in range(1, count):
        total = total + sums[source]
    across = jnp.sum(total, axis=1, keepdims=True)
    moments = [jnp.broadcast_to(across[m : m + 1, :], (SUB, LANES)) for m in range(2 * ITERS)]
    solved, sound = solve_coefficients(moments)
    sound_out[0] = jnp.min(jnp.where(sound, 1, 0))

    def mixed(parts):
        return functools.reduce(jnp.add, [a * p for a, p in zip(solved, parts, strict=True)])

    for c in range(cols // LANES):
        cut = pl.ds(LANES * c, LANES)

        def at_edge(side, row):
            return mixed([edge[k, side, pl.ds(row, SUB), cut] for k in range(ITERS)])

        halo[0:SUB, cut] = at_edge(0, 0)
        field[0:SUB, cut] = at_edge(0, SUB)
        field[rows - SUB : rows, cut] = at_edge(1, 0)
        halo[SUB : 2 * SUB, cut] = at_edge(1, SUB)
        for start in range(SUB, rows - SUB, SUB):
            at = pl.ds(SUB + start, SUB)
            field[pl.ds(start, SUB), cut] = mixed([inner[k, at, cut] for k in range(ITERS)])
    fill_sent(slot_of, field, side_theta, side_weight, end_theta, end_weight, sent, lines)


def tracer_kernel(
    thickness, widths, field, halo, near, far, theta2, diffusivity, mask,
    out, free_out, theta_all, spread_all, mask_all, scaled, roots, beyond, in_sems, out_sems,
):
    me = lax.axis_index("gx")
    count = lax.axis_size("gx")
    levels, rows, cols = theta2.shape
    wide = cols // LANES
    even = lax.rem(me, 2) == 0
    lane, _ = tile_iotas()
    west_rate, east_rate, south_rate, north_rate = side_rates(widths, me, count, rows)

    def loads(l):
        pairs = ((theta2, theta_all), (diffusivity, spread_all), (mask, mask_all))
        return [
            pltpu.make_async_copy(a.at[l], b.at[l], in_sems.at[i, l])
            for i, (a, b) in enumerate(pairs)
        ]

    def store(l):
        return pltpu.make_async_copy(theta_all.at[l], out.at[l], out_sems.at[l])

    for l in range(levels):
        for copy in loads(l):
            copy.start()
    free_copy = pltpu.make_async_copy(field, free_out, out_sems.at[levels])
    free_copy.start()

    for side in range(2):
        mine, other = (far, near) if side == 0 else (near, far)
        theta_row = jnp.where(even, mine[0:levels, :], other[0:levels, :])
        root_row = jnp.where(even, mine[levels : 2 * levels, :], other[levels : 2 * levels, :])
        line = SUB - 1 if side == 0 else SUB
        free = halo[line : line + 1, :]
        deep = jnp.concatenate([thickness[l] * free for l in range(levels)], axis=0)
        total = theta_row + jnp.where(root_row > 0.0, deep, 0.0)
        line_lane = lax.broadcasted_iota(jnp.int32, (levels, cols), 1)
        gamma = rate(line_lane, widths, 0) + rate(cols - 1 - line_lane, widths, 1)
        lines = root_row * ((1.0 - gamma) * total)
        for l in range(levels):
            beyond[side, l] = lines[l : l + 1, :]

    @pl.loop(0, levels)
    def _(level):
        for copy in loads(level):
            copy.wait()
        scaled[SUB - 1 : SUB, :] = beyond[0, level]
        scaled[SUB + rows : SUB + rows + 1, :] = beyond[1, level]
        weight = thickness[level]
        for start in range(0, rows, SUB):
            for c in range(wide):
                at = (pl.ds(start, SUB), pl.ds(LANES * c, LANES))
                wet = mask_all[(level, *at)] != 0
                total = theta_all[(level, *at)] + jnp.where(wet, weight * field[at], 0.0)
                parts = [
                    r
                    for r, there in (
                        (west_rate, c == 0),
                        (east_rate, c == wide - 1),
                        (south_rate, start == 0),
                        (north_rate, start == rows - SUB),
                    )
                    if there
                ]
                one = total
                if parts:
                    one = jnp.where(wet, 1.0 - functools.reduce(jnp.add, parts), 1.0) * total
                spread = spread_all[(level, *at)].astype(f32)
                root = jnp.where(wet, spread * lax.rsqrt(spread), 0.0)
                theta_all[(level, *at)] = one
                roots[at] = root
                scaled[pl.ds(SUB + start, SUB), pl.ds(LANES * c, LANES)] = root * one
        for start in range(0, rows, SUB):
            here = tiles_of(scaled, (), SUB + start, wide)
            north = tiles_of(scaled, (), SUB + start - 1, wide)
            south = tiles_of(scaled, (), SUB + start + 1, wide)
            west, east = beside_tiles(here, lane)
            for c in range(wide):
                at = (pl.ds(start, SUB), pl.ds(LANES * c, LANES))
                ring = (north[c] + south[c]) + (west[c] + east[c])
                theta_all[(level, *at)] += roots[at] * (ring - 4.0 * here[c])
        store(level).start()

    free_copy.wait()
    for l in range(levels):
        store(l).wait()


def rim_kernel(got, rim):
    count, height, _ = got.shape
    levels, width = rim.shape
    total = got[0]
    for source in range(1, count):
        total = total + got[source]
    square = jnp.concatenate([total, jnp.zeros((LANES - height, LANES), f32)], axis=0)
    spread = (
        lax.broadcasted_iota(jnp.int32, (LANES, width), 1) // SEG
        == lax.broadcasted_iota(jnp.int32, (LANES, width), 0)
    ).astype(jnp.bfloat16)
    wide = exact_dot(spread, square.T, "values first")
    phase = lax.rem(lax.broadcasted_iota(jnp.int32, (SUB, width), 1), SEG)
    sub = lax.broadcasted_iota(jnp.int32, (SUB, width), 0)
    for l in range(levels):
        cells = jnp.where(phase == sub, wide[SUB * l : SUB * (l + 1), :], 0.0)
        rim[l : l + 1, :] = jnp.sum(cells, axis=0, keepdims=True)


VMEM = pl.BlockSpec(memory_space=pltpu.VMEM)
SMEM = pl.BlockSpec(memory_space=pltpu.SMEM)
ANY = pl.BlockSpec(memory_space=pl.ANY)


def whole(shape):
    return pl.BlockSpec(shape, lambda *_: (0,) * len(shape))


def local_call(kernel, name, outs, ins, out_specs=None, scratch=(), limit=16, **more):
    return pl.pallas_call(
        kernel,
        out_shape=tuple(jax.ShapeDtypeStruct(*o) if isinstance(o, tuple) else o for o in outs),
        in_specs=ins,
        out_specs=out_specs or tuple(VMEM for _ in outs),
        scratch_shapes=list(scratch),
        compiler_params=pltpu.CompilerParams(vmem_limit_bytes=limit * 2**20),
        name=name,
        **more,
    )


def shards(
    adj_theta2, adj_eta, diffusivity, land_mask, surface_coef, thickness, seg_perm, sponge_width
):
    levels, rows, cols = adj_theta2.shape
    count = lax.axis_size("gx")
    me = lax.axis_index("gx")
    even = lax.rem(me, 2) == 0
    local_segs = (2 * rows * count + 2 * cols) // SEG // count
    slots = -(-local_segs // SUB) * SUB
    slot_of = seg_perm // local_segs * slots + seg_perm % local_segs
    inner_pairs = [(i, i ^ 1) for i in range(count)]
    outer_pairs = [p for i in range(1, count - 1, 2) for p in ((i, i + 1), (i + 1, i))]

    def edges(at_end):
        start = jnp.where(at_end, rows - ITERS, 0)
        return jnp.concatenate(
            [lax.dynamic_slice_in_dim(a, start, ITERS, 0) for a in (adj_eta, surface_coef)]
        )

    fields = [
        pltpu.with_memory_space_constraint(a, pltpu.HBM)
        for a in (adj_eta, surface_coef, adj_theta2, diffusivity, land_mask)
    ]
    first = lax.ppermute(edges(even), "gx", inner_pairs)
    second = lax.ppermute(edges(jnp.logical_not(even)), "gx", outer_pairs)

    inner, diag, partial, near, far, *parts = local_call(
        ready_kernel,
        "ready",
        [
            ((ITERS, rows + 2 * SUB, cols), f32),
            ((rows, cols), f32),
            ((2 * ITERS, SUB, LANES), f32),
            ((2 * levels, cols), f32),
            ((2 * levels, cols), f32),
            pltpu.VMEM((2, rows, LANES), f32),
            pltpu.VMEM((2, rows, LANES), f32),
            pltpu.VMEM((levels, cols), f32),
            pltpu.VMEM((levels, SUB, cols), f32),
        ],
        [SMEM, SMEM, ANY, ANY, ANY, ANY, ANY],
        scratch=[
            pltpu.VMEM((2, levels, SUB, cols), f32),
            pltpu.VMEM((2, levels, SUB, cols), jnp.int32),
            pltpu.VMEM((2, levels, 2 * SUB, cols), diffusivity.dtype),
            pltpu.VMEM((2, levels, rows, LANES), f32),
            pltpu.VMEM((2, levels, rows, LANES), jnp.int32),
            pltpu.SemaphoreType.DMA((6,)),
            pltpu.SemaphoreType.DMA((4,)),
            pltpu.SemaphoreType.DMA((2,)),
        ],
        cost_estimate=pl.CostEstimate(flops=10**6, bytes_accessed=4 * 10**6, transcendentals=0),
    )(thickness, sponge_width, *fields)
    edge, sums = local_call(
        outer_kernel,
        "outer",
        [((ITERS, 2, 2 * SUB, cols), f32), pltpu.HBM((count, 2 * ITERS, LANES), f32)],
        [VMEM] * 5,
        scratch=[pltpu.VMEM((ITERS, 2, 4 * SUB, cols), f32), pltpu.VMEM((2, 4 * SUB, cols), f32)],
    )(inner, diag, partial, first, second)
    sums, near, far = lax.optimization_barrier((sums, near, far))
    all_sums = lax.all_to_all(sums, "gx", 0, 0)
    near = lax.ppermute(near, "gx", inner_pairs)
    far = lax.ppermute(far, "gx", outer_pairs)

    sent_shape = pltpu.HBM((count * slots, LANES), f32)
    sent_scratch = [pltpu.VMEM((cols // SEG, LANES), f32)]
    field, halo, sent, sound = local_call(
        field_kernel,
        "field",
        [
            pltpu.VMEM((rows, cols), f32),
            ((2 * SUB, cols), f32),
            sent_shape,
            ((1,), jnp.int32),
        ],
        [SMEM] + [VMEM] * 7,
        out_specs=(VMEM, VMEM, VMEM, SMEM),
        scratch=sent_scratch,
    )(slot_of, all_sums, inner, edge, *parts)

    def route(rows_out):
        got = lax.all_to_all(rows_out.reshape(count, slots, LANES), "gx", 0, 0)
        (adj_rim,) = local_call(
            rim_kernel, "rim", [pltpu.HBM((levels, local_segs * SEG), f32)], [VMEM]
        )(got)
        return adj_rim

    def tracer(free, beyond):
        return local_call(
            tracer_kernel,
            "tracer",
            [pltpu.HBM((levels, rows, cols), f32), pltpu.HBM((rows, cols), f32)],
            [SMEM] * 2 + [VMEM] * 4 + [ANY] * 3,
            out_specs=(ANY, ANY),
            scratch=[
                pltpu.VMEM((levels, rows, cols), f32),
                pltpu.VMEM((levels, rows, cols), diffusivity.dtype),
                pltpu.VMEM((levels, rows, cols), jnp.int32),
                pltpu.VMEM((rows + 2 * SUB, cols), f32),
                pltpu.VMEM((rows, cols), f32),
                pltpu.VMEM((2, levels, 1, cols), f32),
                pltpu.SemaphoreType.DMA((3, levels)),
                pltpu.SemaphoreType.DMA((levels + 1,)),
            ],
            cost_estimate=pl.CostEstimate(
                flops=24 * 10**6, bytes_accessed=12 * 10**6, transcendentals=10**6
            ),
        )(
            thickness, sponge_width, free, beyond, near, far, *fields[2:]
        )

    sent, near, far = lax.optimization_barrier((sent, near, far))
    adj_rim = route(sent)
    adj_theta, adj_free = tracer(field, halo)

    def again():
        free, beyond = plain_solve(adj_eta, surface_coef)
        (rows_out,) = local_call(
            fill_sent, "refill", [sent_shape], [SMEM] + [VMEM] * 5, scratch=sent_scratch
        )(slot_of, free, *parts)
        return *tracer(free, beyond), route(rows_out)

    return lax.cond(sound[0] > 0, lambda: (adj_theta, adj_free, adj_rim), again)


def solution(mesh):
    return jax.shard_map(
        shards,
        mesh=mesh,
        in_specs=(
            P("member", "gx", None),
            P(("member", "gx"), None),
            P(None, "gx", None),
            P(None, "gx", None),
            P("gx", None),
            P(),
            P(),
            P(),
        ),
        out_specs=(P("member", "gx", None), P(("member", "gx"), None), P("member", "gx")),
        check_vma=False,
    )
```
